512 devices in a mesh: dp: 16 (over y, core), seq: 32 (over x, z).
Axes of the slice: x: 4, y: 8, z: 8, core: 2. Of those that a mesh axis runs over, the one named last changes fastest.
Arguments:
- tokens: bfloat16 [8192, 4096], P('seq', 'dp'), may hold values from -6 to 6
- mask_flags: int32 [8192], P('seq'), may hold values 0 or 1
- doc_lengths: int32 [64], replicated, may hold values from 1 to 6144, 8192 in all
- mask_embed: bfloat16 [4096], P('dp'), may hold values from -6 to 6
- norm_gain: bfloat16 [4096], replicated, may hold values from 0.099609375 to 1.8984375
- qkv_weight: bfloat16 [4096, 16, 384], P(None, 'dp'), may hold values from -0.09375 to 0.09375
- out_weight: bfloat16 [16, 128, 4096], P('dp'), may hold values from -0.1875 to 0.1875
Outputs:
- mixed: bfloat16 [8192, 4096], P('seq', 'dp')
The draws below stay inside these ranges and needn't reach their ends.
Inputs may be any that keep to these rules, and one draw needn't show every extreme that they name: `doc_lengths`: document lengths sum to 8192; the longest has exactly 6144 tokens.
All inputs are finite; a program needn't handle non-finite values. No bound on the sum of `mask_flags` on one device may be relied on, other than what follows from the above.
Results may differ from the reference program's by a relative error of at most 0.0045.
The reference program's roundings to bfloat16 on the way (of `masked`, `scaled`, `projected`, `weights_low` and `attended`) count: a program that leaves them out, or rounds other values in their place, can miss the bound.
Values may be sent and summed in bfloat16 or wider, within the bound.
A program may use at most 64 MiB of HBM per device.

```python
import math
import jax
import jax.numpy as jnp
import numpy as np
from jax import lax

D = 4096
HD = 128
HEADS = 16
TOKCOL = 256
TOKENS = 8192
DOCS = 64
DOC_MOST = 6144
N_SEQ = 32


def plant(result, own_key, smallest, largest):
    longest = result.shape.index(max(result.shape))
    spots = []
    for shift in (0, 1):
        where = [jax.random.randint(jax.random.fold_in(own_key, axis), (), 0, length) for axis, length in enumerate(result.shape)]
        where[longest] = (where[longest] + shift) % result.shape[longest]
        spots.append(tuple(where))
    return result.at[spots[0]].set(smallest).at[spots[1]].set(largest)


def strengthened(drawn, own_key, source, target, shards_of, factor):
    def block_of(axis_at):
        return (jnp.arange(drawn.shape[axis_at]) // (drawn.shape[axis_at] // shards_of)).reshape((-1,) + (1,) * (drawn.ndim - 1 - axis_at))

    one_side = jax.random.permutation(own_key, shards_of)[block_of(target)]
    far = (block_of(target) + shards_of // 2) % shards_of
    return jnp.where((block_of(source) == one_side) | (block_of(source) == far), factor * drawn, drawn)


def levels(rng, dims, split, least, top_value):
    def one(dim, shards_of):
        heights = jax.random.uniform(jax.random.fold_in(jax.random.fold_in(rng, 6), dim), (shards_of,), jnp.float32, least / len(split), top_value / len(split))
        return jnp.repeat(jnp.exp(heights), dims[dim] // shards_of).reshape((-1,) + (1,) * (len(dims) - dim - 1))

    gain = one(*split[0])
    for cut in split[1:]:
        gain = gain * one(*cut)
    return gain


def split_up(amount, total, reach, skew):
    weights = [(1 << 20) // math.isqrt(rank ** skew) + 1 for rank in range(2, amount + 1)]
    surplus, holding = total - reach - (amount - 1), [1] * (amount - 1)
    while surplus > 0:
        free = [i for i in range(amount - 1) if holding[i] < reach]
        mass, budget = sum([weights[i] for i in free]), surplus
        for i in free:
            more = min(reach - holding[i], max(1, budget * weights[i] // mass), surplus)
            holding[i] = holding[i] + more
            surplus = surplus - more
    return np.array([reach] + holding)


def uneven_parts(own_key, number_of, total, reach, skew):
    if number_of == 2:
        one = jax.random.randint(own_key, (), max(1, total - reach), min(reach, total - 1) + 1)
        return jnp.stack([one, total - one])
    tallies = jnp.asarray(split_up(number_of, total, reach, skew), jnp.int32)
    twos = (number_of - 1) // 2
    donor, sink = tallies[1:1 + 2 * twos:2], tallies[2:2 + 2 * twos:2]
    slack = jnp.minimum(donor - 1, reach - sink)
    shifted = jax.random.randint(jax.random.fold_in(own_key, 1), (twos,), 0, 1 << 20) % (slack + 1)
    tallies = tallies.at[1:1 + 2 * twos:2].set(donor - shifted).at[2:2 + 2 * twos:2].set(sink + shifted)
    return tallies[jax.random.permutation(jax.random.fold_in(own_key, 2), number_of)]


def centred(stream_key, extent, spread, most, split=(), held_as=jnp.bfloat16):
    factor_of = levels(stream_key, extent, split, -0.22, 0.18) if split else 1.0
    entries = jax.random.normal(stream_key, extent, jnp.float32) * spread * factor_of
    return jnp.minimum(jnp.maximum(entries, -most), most).astype(held_as)


def bell_draw_with(rng, dims, spread, bound, shards, heavy, held_as=jnp.bfloat16):
    result = spread * jax.random.normal(rng, dims, jnp.float32)
    if shards:
        result = result * levels(rng, dims, shards, -0.22, 0.18)
    return jnp.clip(strengthened(result, jax.random.fold_in(rng, 3), *heavy), -bound, bound).astype(held_as)


def setup_inputs(seed: int = 0) -> dict:
    seeds = jax.random.split(jax.random.key(seed), 8)
    return {
        "tokens": centred(seeds[0], (TOKENS, D), 1.0, 6.0, ((0, 32), (1, 16))),
        "mask_flags": plant((jax.random.randint(seeds[1], (TOKENS,), 0, 2) < 1).astype(jnp.int32), jax.random.fold_in(seeds[1], 1), 0, 1),
        "doc_lengths": uneven_parts(seeds[2], DOCS, TOKENS, DOC_MOST, 2).astype(jnp.int32),
        "mask_embed": centred(seeds[3], (D,), 1.0, 6.0, ((0, 16),)),
        "norm_gain": jnp.clip(1.0 + 0.18 * jax.random.normal(seeds[4], (D,), jnp.float32), 0.099609375, 1.8984375).astype(jnp.bfloat16),
        "qkv_weight": centred(seeds[5], (D, HEADS, 3 * HD), D ** -0.5, 0.09375, ((1, 16),)),
        "out_weight": bell_draw_with(seeds[6], (HEADS, HD, D), (HEADS * HD) ** -0.5, 0.1875, ((0, 16),), (0, 2, 16, 2.0)),
    }


def segments_of(position, doc_lengths):
    doc_ends = jnp.cumsum(doc_lengths).astype(jnp.int32)
    return lax.optimization_barrier(jnp.sum((position[:, None] >= doc_ends[None, :]).astype(jnp.int32), axis=1)).astype(jnp.int32)

def reference(tokens, mask_flags, doc_lengths, mask_embed, norm_gain, qkv_weight, out_weight):
    masked = jnp.where(mask_flags[:, None] == 1, mask_embed[None, :], tokens)
    values = masked.astype(jnp.float32)
    inv_rms = lax.rsqrt(lax.optimization_barrier(jnp.mean(values * values, axis=1, keepdims=True)) + 1e-05)
    scaled = (values * norm_gain.astype(jnp.float32)[None, :]).astype(jnp.bfloat16)
    projected = jnp.dot(scaled, qkv_weight.reshape(D, HEADS * 3 * HD), preferred_element_type=jnp.float32)
    projected = (projected * inv_rms).astype(jnp.bfloat16).reshape(TOKENS, HEADS, 3, HD)
    queries = projected[:, :, 0, :]
    key_rows = projected[:, :, 1, :].astype(jnp.float32)
    value_rows = projected[:, :, 2, :].astype(jnp.float32)
    segment = segments_of(jnp.arange(TOKENS, dtype=jnp.int32), doc_lengths)
    factor = 1.0 / math.sqrt(HD)

    def one_block(block_args):
        query_block, segment_block = block_args
        scores = jnp.einsum('qhd,khd->hqk', query_block.astype(jnp.float32), key_rows) * factor
        same_doc = segment_block[:, None] == segment[None, :]
        weights = jnp.where(same_doc[None], jnp.exp(scores), 0.0)
        weights_low = lax.optimization_barrier(weights.astype(jnp.bfloat16)).astype(jnp.float32)
        numerator = jnp.einsum('hqk,khd->qhd', weights_low, value_rows)
        denominator = lax.optimization_barrier(jnp.sum(weights, axis=2)).T
        return (numerator / denominator[:, :, None]).astype(jnp.bfloat16)
    attended = lax.map(one_block, (queries.reshape(N_SEQ, TOKCOL, HEADS, HD), segment.reshape(N_SEQ, TOKCOL)))
    attended = attended.reshape(TOKENS, HEADS * HD)
    mixed = jnp.dot(attended, out_weight.reshape(HEADS * HD, D), preferred_element_type=jnp.float32)
    return mixed.astype(jnp.bfloat16)
```

```python
import math

import jax
import jax.numpy as jnp
from jax import lax
from jax.experimental import pallas as pl
from jax.experimental.pallas import tpu as pltpu
from jax.sharding import PartitionSpec as P

NY, NX, NZ = 8, 4, 8
ROWS, FEAT, HD, HEADS, D = 256, 256, 128, 16, 4096
NC = 2
R = ROWS // NC
H = R // 2
F32, BF16 = jnp.float32, jnp.bfloat16
SCALE = math.log2(math.e) / math.sqrt(HD)


def remote(src, dst, send, recv, dp, seq):
    return pltpu.make_async_remote_copy(
        src_ref=src, dst_ref=dst, send_sem=send, recv_sem=recv,
        device_id=(dp, seq), device_id_type=pl.DeviceIdType.MESH,
    )


class Ring:
    def __init__(self, slot, send, recv, up, down, c):
        self.slot, self.send, self.recv, self.up, self.down, self.c = slot, send, recv, up, down, c
        self.copies = {}

    def go(self, direction, s):
        to = s + 1 if direction == "up" else (s - 1) % 8
        half = None
        if to == 4:
            half = 0 if direction == "up" else 1
        sem = 8 if to == 4 and direction == "down" else to
        copy = remote(
            self.slot(s, half), self.slot(to, half), self.send.at[self.c, sem], self.recv.at[self.c, sem],
            *(self.up if direction == "up" else self.down),
        )
        copy.start()
        self.copies[sem] = copy

    def arrived(self, direction, t):
        sem = t if direction == "up" else (8 if t == 4 else 8 - t)
        self.copies[sem].wait_recv()

    def finish(self):
        for copy in self.copies.values():
            copy.wait_send()


class Pair:
    def __init__(self, mine, theirs, send, recv, other, c):
        self.mine, self.theirs, self.send, self.recv, self.other, self.c = mine, theirs, send, recv, other, c
        self.copies = {}

    def go(self, s):
        copy = remote(self.mine(s), self.theirs(s), self.send.at[self.c, s], self.recv.at[self.c, s], *self.other)
        copy.start()
        self.copies[s] = copy

    def arrived(self, s):
        self.copies[s].wait_recv()

    def finish(self):
        for copy in self.copies.values():
            copy.wait_send()


def kernel(
    tokens, flags, lens, embed, gain, wqkv, wout, out,
    tokin, tok, w, kv, q, numer, den, redo, redi, att, wb, acc, ssq, segq, segk,
    local, ysend, yrecv, bsend, brecv, zsend, zrecv, qsend, qrecv, rsend, rrecv,
    asend, arecv, csend, crecv, was, war, wbs, wbr, wcs, wcr,
):
    dp, seq = lax.axis_index("dp"), lax.axis_index("seq")
    y, core = dp // 2, lax.rem(dp, 2)
    x, z = seq // NZ, lax.rem(seq, NZ)

    load_tok = pltpu.make_async_copy(tokens, tokin, local.at[0])
    load_w = pltpu.make_async_copy(wqkv, w, local.at[1])
    load_tok.start()
    load_w.start()

    def dp_at(dy, c):
        return lax.rem(y + dy + NY, NY) * 2 + c

    def seq_at(dx, dz):
        return lax.rem(x + dx + NX, NX) * NZ + lax.rem(z + dz + NZ, NZ)

    barrier = pltpu.get_barrier_semaphore()

    @pl.loop(1, HEADS)
    def _(k):
        pl.semaphore_signal(
            barrier, inc=1, device_id=(lax.rem(dp + k, HEADS), seq), device_id_type=pl.DeviceIdType.MESH
        )

    @pl.loop(1, NZ)
    def _(k):
        pl.semaphore_signal(barrier, inc=1, device_id=(dp, seq_at(0, k)), device_id_type=pl.DeviceIdType.MESH)

    @pl.loop(1, NX)
    def _(k):
        pl.semaphore_signal(barrier, inc=1, device_id=(dp, seq_at(k, 0)), device_id_type=pl.DeviceIdType.MESH)

    load_tok.wait()
    embed_row = embed[...].astype(F32)
    for c in range(NC):
        rows = pl.ds(c * R, R)
        flag = jnp.transpose(jnp.broadcast_to(flags[c : c + 1, :].astype(F32), (R, R)))
        flag = jnp.concatenate([flag, flag], axis=1)
        masked = jnp.where(flag == 1.0, embed_row, tokin[rows, :].astype(F32))
        tok[0, 0, rows, :] = masked.astype(BF16)

    pl.semaphore_wait(barrier, HEADS - 1 + NZ - 1 + NX - 1)

    up_y, down_y = (dp_at(1, core), seq), (dp_at(-1, core), seq)
    up_z, down_z = (dp, seq_at(0, 1)), (dp, seq_at(0, -1))
    sibling = (y * 2 + 1 - core, seq)

    def part(c, half):
        return pl.ds(c * R, R) if half is None else pl.ds(c * R + half * H, H)

    token_ring = [
        Ring(lambda s, half, c=c: tok.at[0, s, part(c, half)], ysend, yrecv, up_y, down_y, c) for c in range(NC)
    ]
    token_pair = [
        Pair(lambda s, c=c: tok.at[0, s, part(c, None)], lambda s, c=c: tok.at[1, s, part(c, None)],
             bsend, brecv, sibling, c) for c in range(NC)
    ]
    kv_ring = [
        Ring(lambda s, half, c=c: kv.at[s, part(c, half)], zsend, zrecv, up_z, down_z, c) for c in range(NC)
    ]
    att_ring = [
        Ring(lambda s, half, c=c: att.at[0, s, part(c, half)], asend, arecv, up_y, down_y, c) for c in range(NC)
    ]
    att_pair = [
        Pair(lambda s, c=c: att.at[0, s, part(c, None)], lambda s, c=c: att.at[1, s, part(c, None)],
             csend, crecv, sibling, c) for c in range(NC)
    ]

    def own_tokens(c):
        token_ring[c].go("up", 0)
        token_ring[c].go("down", 0)

    own_tokens(0)
    for c in range(NC):
        token_pair[c].go(0)

    holder = lax.rem(dp, NX) == x
    hq = dp // NX

    def out_tile(d):
        return wout.at[0, pl.ds(pl.multiple_of(z * 16, 16), 16), pl.ds(pl.multiple_of(d * FEAT, FEAT), FEAT)]

    def first_hop(k):
        d = lax.rem(dp + k, HEADS)
        return remote(out_tile(d), wb.at[x, z, hq], was.at[k], war.at[hq], d, seq)

    own_tile = pltpu.make_async_copy(out_tile(dp), wb.at[x, z, hq], local.at[2])

    @pl.when(holder)
    def _():
        own_tile.start()

        @pl.loop(1, HEADS)
        def _(k):
            first_hop(k).start()

    def second_hop(k):
        return remote(wb.at[x, z], wb.at[x, z], wbs.at[k], wbr.at[k], dp, seq_at(0, k))

    def third_hop(k):
        return remote(wb.at[x], wb.at[x], wcs.at[k], wcr.at[k], dp, seq_at(k, 0))

    def start_second():
        @pl.when(holder)
        def _():
            own_tile.wait()

        @pl.loop(0, HEADS // NX)
        def _(i):
            @pl.when(i * NX + x != dp)
            def _():
                remote(
                    out_tile(dp), wb.at[x, z, i], was.at[0], war.at[i], lax.rem(dp + 1, HEADS), seq
                ).wait_recv()

        @pl.loop(1, NZ)
        def _(k):
            second_hop(k).start()

    def start_third():
        @pl.loop(1, NZ)
        def _(k):
            second_hop(k).wait_recv()

        @pl.loop(1, NX)
        def _(k):
            third_hop(k).start()

    lane = lax.broadcasted_iota(jnp.int32, (HD, HD), 1)
    row = lax.broadcasted_iota(jnp.int32, (HD, HD), 0)
    lens_lane = jnp.broadcast_to(lens[...].astype(F32), (HD, HD))
    lens_row = jnp.transpose(lens_lane)
    ends_lane = jnp.sum(jnp.where(row <= lane, lens_row, 0.0), axis=0, keepdims=True)
    ends_row = jnp.sum(jnp.where(lane <= row, lens_lane, 0.0), axis=1, keepdims=True)
    for s in range(NX):
        base = seq_at(-s, 0) * ROWS
        position = (lax.broadcasted_iota(jnp.int32, (ROWS, HD), 0) + base).astype(F32)
        count = jnp.sum(jnp.where(position >= ends_lane, 1.0, 0.0), axis=1, keepdims=True)
        segq[s] = jnp.broadcast_to(count, (ROWS, HD))
    for s in range(NZ):
        base = seq_at(0, -s) * ROWS
        position = (lax.broadcasted_iota(jnp.int32, (HD, ROWS), 1) + base).astype(F32)
        count = jnp.sum(jnp.where(position >= ends_row, 1.0, 0.0), axis=0, keepdims=True)
        segk[s] = jnp.broadcast_to(count, (8, ROWS))

    numer[...] = jnp.zeros_like(numer)
    den[...] = jnp.zeros_like(den)
    load_w.wait()

    def project(o, s, c):
        rows = pl.ds(c * R, R)
        f = dp_at(-s, core if o == 0 else 1 - core)
        values = tok[o, s, rows, :].astype(F32)
        squares = values * values
        squares = squares[:, :HD] + squares[:, HD:]
        scaled = (values * gain[pl.ds(f, 1), :]).astype(BF16)
        product = jnp.dot(
            scaled, w[pl.ds(pl.multiple_of(f * FEAT, FEAT), FEAT), :], preferred_element_type=F32
        )
        if (o, s) == (0, 0):
            ssq[rows, :] = squares
            acc[rows, :] = product
        else:
            ssq[rows, :] += squares
            acc[rows, :] += product

    q_copies = {}

    def projected(c):
        rows = pl.ds(c * R, R)
        total = jnp.sum(ssq[rows, :], axis=1, keepdims=True)
        inv_rms = lax.rsqrt(total / D + 1e-05)
        values = (acc[rows, :] * inv_rms).astype(BF16)
        kv[0, rows, :] = values[:, HD:]
        q[0, rows, :] = values[:, :HD]
        kv_ring[c].go("up", 0)
        kv_ring[c].go("down", 0)
        for k in range(1, NX):
            copy = remote(q.at[0, rows], q.at[k, rows], qsend.at[c, k], qrecv.at[c, k], dp, seq_at(k, 0))
            copy.start()
            q_copies[c, k] = copy

    def attend(qc, s, c):
        rows = pl.ds(qc * R, R)
        keys = pl.ds(c * R, R)
        queries = q[:, rows, :].reshape(NX * R, HD)
        scores = lax.dot_general(
            queries, kv[s, keys, :HD], (((1,), (1,)), ((), ())), preferred_element_type=F32
        )
        same = segq[:, rows, :].reshape(NX * R, HD) == segk[s, 0:1, keys]
        weights = jnp.where(same, jnp.exp2(scores * SCALE), 0.0)
        product = jnp.dot(weights.astype(BF16), kv[s, keys, HD:], preferred_element_type=F32)
        numer[:, rows, :] += product.reshape(NX, R, HD)
        den[:, rows, :] += weights.reshape(NX, R, HD)

    def token_step(c, t):
        ring, pair = token_ring[c], token_pair[c]
        if t == 0:
            project(0, 0, c)
            return
        ring.arrived("up", t)
        if t < 4:
            ring.go("up", t)
            pair.go(t)
        ring.arrived("down", t)
        if t < 4:
            ring.go("down", 8 - t)
            pair.go(8 - t)
        else:
            pair.go(4)
        project(0, t, c)
        if t < 4:
            project(0, 8 - t, c)
        pair.arrived(t - 1)
        project(1, t - 1, c)
        if t > 1:
            pair.arrived(9 - t)
            project(1, 9 - t, c)
        if t == 4:
            pair.arrived(4)
            project(1, 4, c)

    def kv_step(c, t, chunks):
        ring = kv_ring[c]
        if t == 0:
            for k in range(1, NX):
                q_copies[c, k].wait_recv()
        else:
            ring.arrived("up", t)
            if t < 4:
                ring.go("up", t)
            ring.arrived("down", t)
            if t < 4:
                ring.go("down", 8 - t)
        for qc in chunks:
            attend(qc, t, c)
            if 0 < t < 4:
                attend(qc, 8 - t, c)

    for c in range(NC):
        for t in range(5):
            token_step(c, t)
            if c > 0:
                kv_step(c - 1, t, [c - 1])
            if t == 2:
                if c + 1 < NC:
                    own_tokens(c + 1)
                if c == 0:
                    start_second()
                if c == 1:
                    start_third()
        projected(c)

    last = NC - 1
    for t in range(4):
        kv_step(last, t, range(NC))
        for c in range(last):
            attend(last, t, c)
            attend(last, t + 4, c)
    kv_step(last, 4, range(NC))

    r_copies = {}
    for k in (2, 1, 3):
        redo[k, :ROWS, :] = numer[k]
        for i in range(ROWS // HD):
            part_sum = jnp.sum(jnp.transpose(den[k, pl.ds(i * HD, HD), :]), axis=0, keepdims=True)
            redo[k, pl.ds(ROWS + 8 * i, 8), :] = jnp.broadcast_to(part_sum, (8, HD))
        copy = remote(redo.at[k], redi.at[k], rsend.at[k], rrecv.at[k], dp, seq_at(-k, 0))
        copy.start()
        r_copies[k] = copy
    for k in (1, 3, 2):
        r_copies[k].wait_recv()
    for c in range(NC):
        rows = pl.ds(c * R, R)
        down = jnp.sum(jnp.transpose(den[0, rows, :]), axis=0, keepdims=True)
        for k in range(1, NX):
            down = down + redi[k, pl.ds(ROWS + 8 * c, 8), :][0:1, :]
        down = jnp.transpose(jnp.broadcast_to(down, (HD, HD)))
        top = numer[0, rows, :] + redi[1, rows, :] + redi[2, rows, :] + redi[3, rows, :]
        att[0, 0, rows, :] = (top / down).astype(BF16)
        att_ring[c].go("up", 0)
        att_ring[c].go("down", 0)
        att_pair[c].go(0)

    @pl.loop(1, NX)
    def _(k):
        third_hop(k).wait_recv()

    def mix(o, s, c):
        rows = pl.ds(c * R, R)
        h = dp_at(-s, core if o == 0 else 1 - core)
        weight = wb[lax.rem(h, NX), :, h // NX].reshape(HD, FEAT)
        product = jnp.dot(att[o, s, rows, :], weight, preferred_element_type=F32)
        if (o, s) == (0, 0):
            acc[rows, :FEAT] = product
        else:
            acc[rows, :FEAT] += product

    for t in range(5):
        for c in range(NC):
            ring, pair = att_ring[c], att_pair[c]
            if t > 0:
                ring.arrived("up", t)
                if t < 4:
                    ring.go("up", t)
                    pair.go(t)
                ring.arrived("down", t)
                if t < 4:
                    ring.go("down", 8 - t)
                    pair.go(8 - t)
                else:
                    pair.go(4)
        for c in range(NC):
            pair = att_pair[c]
            mix(0, t, c)
            if 0 < t < 4:
                mix(0, 8 - t, c)
            if t > 0:
                pair.arrived(t - 1)
                mix(1, t - 1, c)
            if t > 1:
                pair.arrived(9 - t)
                mix(1, 9 - t, c)
            if t == 4:
                pair.arrived(4)
                mix(1, 4, c)
    out[...] = acc[:, :FEAT].astype(BF16)

    for c in range(NC):
        for group in (token_ring[c], token_pair[c], kv_ring[c], att_ring[c], att_pair[c]):
            group.finish()
    for copy in list(q_copies.values()) + list(r_copies.values()):
        copy.wait_send()

    @pl.when(holder)
    def _():
        @pl.loop(1, HEADS)
        def _(k):
            first_hop(k).wait_send()

    @pl.loop(1, NZ)
    def _(k):
        second_hop(k).wait_send()

    @pl.loop(1, NX)
    def _(k):
        third_hop(k).wait_send()


def body(tokens, mask_flags, doc_lengths, mask_embed, norm_gain, qkv_weight, out_weight):
    lens = jnp.pad(doc_lengths, (0, HD - doc_lengths.shape[0])).reshape(1, HD)
    vmem = pl.BlockSpec(memory_space=pltpu.VMEM)
    anyw = pl.BlockSpec(memory_space=pl.ANY)
    dma = lambda *shape: pltpu.SemaphoreType.DMA(shape)
    return pl.pallas_call(
        kernel,
        out_shape=jax.ShapeDtypeStruct((ROWS, FEAT), BF16),
        in_specs=[anyw, vmem, vmem, vmem, vmem, anyw, anyw],
        out_specs=vmem,
        scratch_shapes=[
            pltpu.VMEM((ROWS, FEAT), BF16),
            pltpu.VMEM((2, NY, ROWS, FEAT), BF16),
            pltpu.VMEM((D, 3 * HD), BF16),
            pltpu.VMEM((NZ, ROWS, 2 * HD), BF16),
            pltpu.VMEM((NX, ROWS, HD), BF16),
            pltpu.VMEM((NX, ROWS, HD), F32),
            pltpu.VMEM((NX, ROWS, HD), F32),
            pltpu.VMEM((NX, ROWS + 16, HD), F32),
            pltpu.VMEM((NX, ROWS + 16, HD), F32),
            pltpu.VMEM((2, NY, ROWS, HD), BF16),
            pltpu.VMEM((NX, NZ, HEADS // NX, 16, FEAT), BF16),
            pltpu.VMEM((ROWS, 3 * HD), F32),
            pltpu.VMEM((ROWS, HD), F32),
            pltpu.VMEM((NX, ROWS, HD), F32),
            pltpu.VMEM((NZ, 8, ROWS), F32),
            dma(3),
            dma(NC, 9), dma(NC, 9), dma(NC, 8), dma(NC, 8),
            dma(NC, 9), dma(NC, 9), dma(NC, NX), dma(NC, NX),
            dma(NX), dma(NX),
            dma(NC, 9), dma(NC, 9), dma(NC, 8), dma(NC, 8),
            dma(HEADS), dma(HEADS // NX), dma(NZ), dma(NZ), dma(NX), dma(NX),
        ],
        compiler_params=pltpu.CompilerParams(
            collective_id=0, has_side_effects=True, vmem_limit_bytes=48 * 1024 * 1024
        ),
        name="attention_layer",
    )(
        tokens, mask_flags.reshape(NC, R), lens, mask_embed.astype(F32).reshape(1, FEAT),
        norm_gain.astype(F32).reshape(HEADS, FEAT), qkv_weight.reshape(D, 3 * HD), out_weight,
    )


def solution(mesh):
    placed = (P("seq", "dp"), P("seq"), P(), P("dp"), P(), P(None, "dp", None), P("dp", None, None))
    return jax.shard_map(
        body, mesh=mesh, in_specs=placed, out_specs=P("seq", "dp"), check_vma=False
    )
```

```python
import math

import jax
import jax.numpy as jnp
from jax import lax
from jax.experimental import pallas as pl
from jax.experimental.pallas import tpu as pltpu
from jax.sharding import PartitionSpec as P

NY, NX, NZ = 8, 4, 8
ROWS, FEAT, HD, HEADS, D, DOCS = 256, 256, 128, 16, 4096, 64
VMEM_BYTES = 63 * 1024 * 1024
H = ROWS // 2
F32, BF16 = jnp.float32, jnp.bfloat16
SCALE = math.log2(math.e) / math.sqrt(HD)


def remote(src, dst, send, recv, dp, seq):
    return pltpu.make_async_remote_copy(
        src_ref=src, dst_ref=dst, send_sem=send, recv_sem=recv,
        device_id=(dp, seq), device_id_type=pl.DeviceIdType.MESH,
    )


CROSS = ((0, 1), (0, -1), (1, 1), (3, -1))
TREE = ((0, 2), (0, -2), (0, 1), (0, -1), (2, 2), (6, -2), (2, 1), (6, -1))


T_PLAN = TREE
KV_PLAN = TREE
ATT_PLAN = TREE


class Ring:
    size = 8

    def __init__(self, plan, slot, send, recv, place):
        self.plan, self.slot, self.send, self.recv, self.place = plan, slot, send, recv, place
        self.copies = {}

    def go(self, s):
        for source, step in self.plan:
            if source == s:
                to = (s + step) % self.size
                half = None if to != self.size // 2 else (0 if step > 0 else 1)
                sem = self.size if half == 1 else to
                copy = remote(
                    self.slot(s, half), self.slot(to, half), self.send.at[sem], self.recv.at[sem],
                    *self.place(step),
                )
                copy.start()
                self.copies[sem] = copy

    def arrived(self, s):
        for sem in (s, self.size) if s == self.size // 2 else (s,):
            self.copies[sem].wait_recv()

    def finish(self):
        for sem, copy in self.copies.items():
            copy.wait_send()


class ShortRing(Ring):
    size = 4


class Pair:
    def __init__(self, mine, theirs, send, recv, other):
        self.mine, self.theirs, self.send, self.recv, self.other = mine, theirs, send, recv, other
        self.copies = {}

    def go(self, s):
        copy = remote(self.mine(s), self.theirs(s), self.send.at[s], self.recv.at[s], *self.other)
        copy.start()
        self.copies[s] = copy

    def arrived(self, s):
        self.copies[s].wait_recv()

    def finish(self):
        for sem, copy in self.copies.items():
            copy.wait_send()


def kernel(
    tokens, flags, lens, embed, gain, wqkv, wout, out,
    tokin, flagin, lenin, embedin, gainin, gain32, tok, w, kv, q, numer, den, redo, redi, dedo, dedi, att, wb, acc, ssq, segq, segk,
    local, ysend, yrecv, bsend, brecv, zsend, zrecv, qsend, qrecv, rsend, rrecv,
    asend, arecv, csend, crecv, was, war, wbs, wbr, wcs, wcr,
):
    dp, seq = lax.axis_index("dp"), lax.axis_index("seq")
    y, core = dp // 2, lax.rem(dp, 2)
    x, z = seq // NZ, lax.rem(seq, NZ)

    loads = [
        pltpu.make_async_copy(there, here, local.at[i])
        for i, (there, here) in enumerate(
            [(tokens, tokin), (flags, flagin), (embed, embedin), (gain, gainin), (lens, lenin), (wqkv, w)]
        )
    ]
    for load in loads:
        load.start()

    def dp_at(dy, c):
        return lax.rem(y + dy + NY, NY) * 2 + c

    def seq_at(dx, dz):
        return lax.rem(x + dx + NX, NX) * NZ + lax.rem(z + dz + NZ, NZ)

    barrier = pltpu.get_barrier_semaphore()

    @pl.loop(1, HEADS)
    def _(k):
        pl.semaphore_signal(
            barrier, inc=1, device_id=(lax.rem(dp + k, HEADS), seq), device_id_type=pl.DeviceIdType.MESH
        )

    @pl.loop(1, NZ)
    def _(k):
        pl.semaphore_signal(barrier, inc=1, device_id=(dp, seq_at(0, k)), device_id_type=pl.DeviceIdType.MESH)

    @pl.loop(1, NX)
    def _(k):
        pl.semaphore_signal(barrier, inc=1, device_id=(dp, seq_at(k, 0)), device_id_type=pl.DeviceIdType.MESH)

    for load in loads[:3]:
        load.wait()
    embed_row = jnp.concatenate([embedin[0:1, :], embedin[1:2, :]], axis=1).astype(F32)
    for c in range(ROWS // HD):
        rows = pl.ds(c * HD, HD)
        flag = jnp.transpose(jnp.broadcast_to(flagin[c : c + 1, :].astype(F32), (HD, HD)))
        flag = jnp.concatenate([flag, flag], axis=1)
        masked = jnp.where(flag == 1.0, embed_row, tokin[rows, :].astype(F32))
        tok[0, 0, rows, :] = masked.astype(BF16)

    pl.semaphore_wait(barrier, HEADS - 1 + NZ - 1 + NX - 1)

    def along_y(step):
        return dp_at(step, core), seq

    def along_z(step):
        return dp, seq_at(0, step)

    sibling = (y * 2 + 1 - core, seq)

    def along_x(step):
        return dp, seq_at(step, 0)

    def rows_of(half):
        return pl.ds(0, ROWS) if half is None else pl.ds(half * H, H)

    token_ring = Ring(T_PLAN, lambda s, half: tok.at[0, s, rows_of(half)], ysend, yrecv, along_y)
    token_pair = Pair(lambda s: tok.at[0, s], lambda s: tok.at[1, s], bsend, brecv, sibling)
    kv_ring = Ring(KV_PLAN, lambda s, half: kv.at[s, rows_of(half)], zsend, zrecv, along_z)
    att_ring = Ring(ATT_PLAN, lambda s, half: att.at[0, s, rows_of(half)], asend, arecv, along_y)
    att_pair = Pair(lambda s: att.at[0, s], lambda s: att.at[1, s], csend, crecv, sibling)

    def weight_part(s, half):
        return wb.at[s] if half is None else wb.at[s, pl.ds(half * (NZ // 2), NZ // 2)]

    weight_ring = ShortRing(CROSS, weight_part, wcs, wcr, along_x)

    turn = lax.rem(x - dp + HEADS, NX)

    def out_tile(d):
        return wout.at[0, pl.ds(pl.multiple_of(z * 16, 16), 16), pl.ds(pl.multiple_of(d * FEAT, FEAT), FEAT)]

    def first_hop(i):
        d = NX * i + turn
        return remote(out_tile(d), wb.at[0, z, dp // NX], was.at[i], war.at[dp // NX], d, seq)

    own_tile = pltpu.make_async_copy(out_tile(dp), wb.at[0, z, dp // NX], local.at[6])

    def second_hop(k):
        return remote(wb.at[0, z], wb.at[0, z], wbs.at[k], wbr.at[k], dp, seq_at(0, k))


    def start_first():
        for i in range(HEADS // NX):
            @pl.when(NX * i + turn != dp)
            def _():
                first_hop(i).start()

            @pl.when(NX * i + turn == dp)
            def _():
                own_tile.start()

    def finish_first():
        for i in range(HEADS // NX):
            @pl.when(NX * i + turn != dp)
            def _():
                remote(out_tile(dp), wb.at[0, z, i], was.at[i], war.at[i], NX * i + turn, seq).wait_recv()

            @pl.when(NX * i + turn == dp)
            def _():
                own_tile.wait()

    def start_second():
        finish_first()

        @pl.loop(1, NZ)
        def _(k):
            second_hop(k).start()

    def start_third():
        @pl.loop(1, NZ)
        def _(k):
            second_hop(k).wait_recv()

        weight_ring.go(0)

    def project(o, s):
        f = dp_at(-s, core if o == 0 else 1 - core)
        values = tok[o, s].astype(F32)
        squares = values * values
        squares = squares[:, :HD] + squares[:, HD:]
        gains = jnp.concatenate([gain32[pl.ds(2 * f, 1), :], gain32[pl.ds(2 * f + 1, 1), :]], axis=1)
        scaled = (values * gains).astype(BF16)
        product = jnp.dot(
            scaled, w[pl.ds(pl.multiple_of(f * FEAT, FEAT), FEAT), :], preferred_element_type=F32
        )
        if (o, s) == (0, 0):
            ssq[...] = squares
            acc[...] = product
        else:
            ssq[...] += squares
            acc[...] += product

    q_copies = {}

    def projected():
        total = jnp.sum(ssq[...], axis=1, keepdims=True)
        inv_rms = lax.rsqrt(total / D + 1e-05)
        kv[0] = (acc[:, HD:] * inv_rms).astype(BF16)
        kv_ring.go(0)
        q[0] = (acc[:, :HD] * inv_rms).astype(BF16)
        for k in (2, 1, 3):
            copy = remote(q.at[0], q.at[k], qsend.at[k], qrecv.at[k], dp, seq_at(k, 0))
            copy.start()
            q_copies[k] = copy

    def attend(xs, s):
        scores = lax.dot_general(
            q[xs], kv[s, :, :HD], (((1,), (1,)), ((), ())), preferred_element_type=F32
        )
        queries = segq[xs]
        same = jnp.concatenate([queries, queries], axis=1) == segk[s, 0:1, :]
        weights = jnp.where(same, jnp.exp2(scores * SCALE), 0.0)
        product = jnp.dot(weights.astype(BF16), kv[s, :, HD:], preferred_element_type=F32)
        lanes = weights[:, :HD] + weights[:, HD:]
        if s == 0:
            numer[xs] = product
            den[xs] = lanes
        else:
            numer[xs] += product
            den[xs] += lanes

    def tokens_in(slots):
        for t in slots:
            token_ring.arrived(t)
            token_ring.go(t)
            token_pair.go(t)

    def project_mine(slots):
        for t in slots:
            project(0, t)

    def project_theirs(slots):
        for t in slots:
            token_pair.arrived(t)
            project(1, t)

    def keys_in(slots):
        for t in slots:
            kv_ring.arrived(t)
            kv_ring.go(t)

    def queries_in():
        for k in range(1, NX):
            q_copies[k].wait_recv()

    def attend_all(places, slots):
        for t in slots:
            for xs in places:
                attend(xs, t)

    def mix(o, s):
        h = dp_at(-s, core if o == 0 else 1 - core)
        weight = wb[lax.rem(x - h - dp + 2 * HEADS, NX), :, h // NX].reshape(HD, FEAT)
        product = jnp.dot(att[o, s], weight, preferred_element_type=F32)
        if (o, s) == (0, 0):
            acc[:, :FEAT] = product
        else:
            acc[:, :FEAT] += product

    def segments():
        loads[3].wait()
        gain32[...] = gainin[...].astype(F32)
        loads[4].wait()
        lane = lax.broadcasted_iota(jnp.int32, (HD, HD), 1)
        row = lax.broadcasted_iota(jnp.int32, (HD, HD), 0)
        lens_lane = jnp.concatenate([lenin[...].astype(F32), jnp.zeros((1, HD - DOCS), F32)], axis=1)
        lens_lane = jnp.broadcast_to(lens_lane, (HD, HD))
        lens_row = jnp.transpose(lens_lane)
        ends_lane = jnp.sum(jnp.where(row <= lane, lens_row, 0.0), axis=0, keepdims=True)
        ends_row = jnp.sum(jnp.where(lane <= row, lens_lane, 0.0), axis=1, keepdims=True)
        for s in range(NX):
            base = seq_at(-s, 0) * ROWS
            position = (lax.broadcasted_iota(jnp.int32, (ROWS, HD), 0) + base).astype(F32)
            count = jnp.sum(jnp.where(position >= ends_lane, 1.0, 0.0), axis=1, keepdims=True)
            segq[s] = jnp.broadcast_to(count, (ROWS, HD))
        for s in range(NZ):
            base = seq_at(0, -s) * ROWS
            position = (lax.broadcasted_iota(jnp.int32, (HD, ROWS), 1) + base).astype(F32)
            count = jnp.sum(jnp.where(position >= ends_row, 1.0, 0.0), axis=0, keepdims=True)
            segk[s] = jnp.broadcast_to(count, (8, ROWS))


    r_copies = {}

    def send_sums(k):
        redo[k] = numer[k].astype(BF16)
        for i in range(ROWS // HD):
            part_sum = jnp.sum(jnp.transpose(den[k, pl.ds(i * HD, HD), :]), axis=0, keepdims=True)
            dedo[k, pl.ds(8 * i, 8), :] = jnp.broadcast_to(part_sum, (8, HD))
        for i, (out_part, in_part) in enumerate(((redo, redi), (dedo, dedi))):
            copy = remote(out_part.at[k], in_part.at[k], rsend.at[i, k], rrecv.at[i, k], dp, seq_at(-k, 0))
            copy.start()
            r_copies[i, k] = copy

    def run():
        start_first()
        token_ring.go(0)
        token_pair.go(0)
        segments()
        loads[5].wait()
        project_mine((0,))
        project_theirs((0,))
        tokens_in((2, 6, 1, 7))
        start_second()
        project_mine((2, 6, 1, 7))
        project_theirs((2, 6, 1, 7))
        tokens_in((3, 5))
        project_mine((3, 5))
        tokens_in((4,))
        project_mine((4,))
        project_theirs((3, 5, 4))
        projected()
        start_third()
        attend(0, 0)
        queries_in()
        attend_all((1, 2, 3), (0,))
        keys_in((2, 6))
        keys_in((1, 7))
        attend_all(range(NX), (2, 6, 1, 7))
        for k in (1, 3):
            weight_ring.arrived(k)
            weight_ring.go(k)
        keys_in((3, 5))
        attend_all(range(NX), (3, 5))
        keys_in((4,))
        for k in (2, 1, 3):
            attend(k, 4)
            send_sums(k)
        attend(0, 4)
        for k in (1, 3, 2):
            for i in range(2):
                r_copies[i, k].wait_recv()
        for c in range(ROWS // HD):
            rows = pl.ds(c * HD, HD)
            down = jnp.sum(jnp.transpose(den[0, rows, :]), axis=0, keepdims=True)
            for k in range(1, NX):
                down = down + dedi[k, pl.ds(8 * c, 8), :][0:1, :]
            down = jnp.transpose(jnp.broadcast_to(down, (HD, HD)))
            top = numer[0, rows, :] + redi[1, rows, :].astype(F32) + redi[2, rows, :].astype(F32)
            top = top + redi[3, rows, :].astype(F32)
            att[0, 0, rows, :] = (top / down).astype(BF16)
        att_ring.go(0)
        att_pair.go(0)
        weight_ring.arrived(2)

        def att_in(slots):
            for t in slots:
                att_ring.arrived(t)
                att_ring.go(t)
                att_pair.go(t)

        def mix_mine(slots):
            for t in slots:
                mix(0, t)

        def mix_theirs(slots):
            for t in slots:
                att_pair.arrived(t)
                mix(1, t)

        mix_mine((0,))
        mix_theirs((0,))
        att_in((2, 6, 1, 7))
        mix_mine((2, 6, 1, 7))
        mix_theirs((2, 6, 1, 7))
        att_in((3, 5))
        mix_mine((3, 5))
        att_in((4,))
        mix_mine((4,))
        mix_theirs((3, 5, 4))
        out[...] = acc[:, :FEAT].astype(BF16)

    run()
    for group in (token_ring, token_pair, kv_ring, att_ring, att_pair, weight_ring):
        group.finish()
    for copy in list(q_copies.values()) + list(r_copies.values()):
        copy.wait_send()

    for i in range(HEADS // NX):
        @pl.when(NX * i + turn != dp)
        def _():
            first_hop(i).wait_send()

    @pl.loop(1, NZ)
    def _(k):
        second_hop(k).wait_send()


def body(tokens, mask_flags, doc_lengths, mask_embed, norm_gain, qkv_weight, out_weight):
    vmem = pl.BlockSpec(memory_space=pltpu.VMEM)
    hbm = pl.BlockSpec(memory_space=pltpu.HBM)
    dma = lambda *shape: pltpu.SemaphoreType.DMA(shape)
    return pl.pallas_call(
        kernel,
        out_shape=jax.ShapeDtypeStruct((ROWS, FEAT), BF16),
        in_specs=[hbm] * 7,
        out_specs=vmem,
        scratch_shapes=[
            pltpu.VMEM((ROWS, FEAT), BF16),
            pltpu.VMEM((ROWS // HD, HD), jnp.int32),
            pltpu.VMEM((1, DOCS), jnp.int32),
            pltpu.VMEM((2, HD), BF16),
            pltpu.VMEM((D // HD, HD), BF16),
            pltpu.VMEM((D // HD, HD), F32),
            pltpu.VMEM((2, NY, ROWS, FEAT), BF16),
            pltpu.VMEM((D, 3 * HD), BF16),
            pltpu.VMEM((NZ, ROWS, 2 * HD), BF16),
            pltpu.VMEM((NX, ROWS, HD), BF16),
            pltpu.VMEM((NX, ROWS, HD), F32),
            pltpu.VMEM((NX, ROWS, HD), F32),
            pltpu.VMEM((NX, ROWS, HD), BF16),
            pltpu.VMEM((NX, ROWS, HD), BF16),
            pltpu.VMEM((NX, 16, HD), F32),
            pltpu.VMEM((NX, 16, HD), F32),
            pltpu.VMEM((2, NY, ROWS, HD), BF16),
            pltpu.VMEM((NX, NZ, HEADS // NX, 16, FEAT), BF16),
            pltpu.VMEM((ROWS, 3 * HD), F32),
            pltpu.VMEM((ROWS, HD), F32),
            pltpu.VMEM((NX, ROWS, HD), F32),
            pltpu.VMEM((NZ, 8, ROWS), F32),
            dma(7),
            dma(9), dma(9), dma(8), dma(8),
            dma(9), dma(9), dma(NX), dma(NX),
            dma(2, NX), dma(2, NX),
            dma(9), dma(9), dma(8), dma(8),
            dma(HEADS // NX), dma(HEADS // NX), dma(NZ), dma(NZ), dma(NX + 1), dma(NX + 1),
        ],
        compiler_params=pltpu.CompilerParams(
            collective_id=0, has_side_effects=True, vmem_limit_bytes=VMEM_BYTES
        ),
        name="attention_layer",
    )(
        tokens, mask_flags.reshape(ROWS // HD, HD), doc_lengths.reshape(1, DOCS), mask_embed.reshape(2, HD),
        norm_gain.reshape(D // HD, HD), qkv_weight.reshape(D, 3 * HD), out_weight,
    )


def solution(mesh):
    placed = (P("seq", "dp"), P("seq"), P(), P("dp"), P(), P(None, "dp", None), P("dp", None, None))
    return jax.shard_map(
        body, mesh=mesh, in_specs=placed, out_specs=P("seq", "dp"), check_vma=False
    )
```

```python
import math

import jax
import jax.numpy as jnp
from jax import lax
from jax.experimental import pallas as pl
from jax.experimental.pallas import tpu as pltpu
from jax.sharding import PartitionSpec as P

NY, NX, NZ = 8, 4, 8
ROWS, FEAT, HD, HEADS, D, DOCS = 256, 256, 128, 16, 4096, 64
VMEM_BYTES = 63 * 1024 * 1024
NC = 2
R = ROWS // NC
H = R // 2
F32, BF16 = jnp.float32, jnp.bfloat16
SCALE = math.log2(math.e) / math.sqrt(HD)


def remote(src, dst, send, recv, dp, seq):
    return pltpu.make_async_remote_copy(
        src_ref=src, dst_ref=dst, send_sem=send, recv_sem=recv,
        device_id=(dp, seq), device_id_type=pl.DeviceIdType.MESH,
    )


CROSS = ((0, 1), (0, -1), (1, 1), (3, -1))
TREE = ((0, 2), (0, -2), (0, 1), (0, -1), (2, 2), (6, -2), (2, 1), (6, -1))


T_PLAN = TREE
KV_PLAN = TREE
ATT_PLAN = TREE


class Ring:
    size = 8

    def __init__(self, plan, slot, send, recv, place):
        self.plan, self.slot, self.send, self.recv, self.place = plan, slot, send, recv, place
        self.copies = {}

    def go(self, s, only=None):
        for source, step in self.plan:
            if source == s and (only is None or abs(step) == only):
                to = (s + step) % self.size
                half = None if to != self.size // 2 else (0 if step > 0 else 1)
                sem = self.size if half == 1 else to
                copy = remote(
                    self.slot(s, half), self.slot(to, half), self.send.at[sem], self.recv.at[sem],
                    *self.place(step),
                )
                copy.start()
                self.copies[sem] = copy

    def arrived(self, s):
        for sem in (s, self.size) if s == self.size // 2 else (s,):
            self.copies[sem].wait_recv()

    def finish(self):
        for sem, copy in self.copies.items():
            copy.wait_send()


class ShortRing(Ring):
    size = 4


class Pair:
    def __init__(self, mine, theirs, send, recv, other):
        self.mine, self.theirs, self.send, self.recv, self.other = mine, theirs, send, recv, other
        self.copies = {}

    def go(self, s):
        copy = remote(self.mine(s), self.theirs(s), self.send.at[s], self.recv.at[s], *self.other)
        copy.start()
        self.copies[s] = copy

    def arrived(self, s):
        self.copies[s].wait_recv()

    def finish(self):
        for sem, copy in self.copies.items():
            copy.wait_send()


def kernel(
    tokens, flags, lens, embed, gain, wqkv, wout, out,
    tokin, flagin, lenin, embedin, gainin, gain32, tok, w, kv, q, numer, den, redo, redi, att, wb, acc, ssq, segq, segk,
    local, ysend, yrecv, bsend, brecv, zsend, zrecv, qsend, qrecv, rsend, rrecv,
    asend, arecv, csend, crecv, was, war, wbs, wbr, wcs, wcr,
):
    dp, seq = lax.axis_index("dp"), lax.axis_index("seq")
    y, core = dp // 2, lax.rem(dp, 2)
    x, z = seq // NZ, lax.rem(seq, NZ)

    loads = [
        pltpu.make_async_copy(there, here, local.at[i])
        for i, (there, here) in enumerate(
            [(tokens, tokin), (flags, flagin), (embed, embedin), (gain, gainin), (lens, lenin), (wqkv, w)]
        )
    ]
    for load in loads:
        load.start()

    def dp_at(dy, c):
        return lax.rem(y + dy + NY, NY) * 2 + c

    def seq_at(dx, dz):
        return lax.rem(x + dx + NX, NX) * NZ + lax.rem(z + dz + NZ, NZ)

    barrier = pltpu.get_barrier_semaphore()

    @pl.loop(1, HEADS)
    def _(k):
        pl.semaphore_signal(
            barrier, inc=1, device_id=(lax.rem(dp + k, HEADS), seq), device_id_type=pl.DeviceIdType.MESH
        )

    @pl.loop(1, NZ)
    def _(k):
        pl.semaphore_signal(barrier, inc=1, device_id=(dp, seq_at(0, k)), device_id_type=pl.DeviceIdType.MESH)

    @pl.loop(1, NX)
    def _(k):
        pl.semaphore_signal(barrier, inc=1, device_id=(dp, seq_at(k, 0)), device_id_type=pl.DeviceIdType.MESH)

    for load in loads[:3]:
        load.wait()
    embed_row = jnp.concatenate([embedin[0:1, :], embedin[1:2, :]], axis=1).astype(F32)
    for c in range(ROWS // HD):
        rows = pl.ds(c * HD, HD)
        flag = jnp.transpose(jnp.broadcast_to(flagin[c : c + 1, :].astype(F32), (HD, HD)))
        flag = jnp.concatenate([flag, flag], axis=1)
        masked = jnp.where(flag == 1.0, embed_row, tokin[rows, :].astype(F32))
        tok[0, 0, rows, :] = masked.astype(BF16)

    pl.semaphore_wait(barrier, HEADS - 1 + NZ - 1 + NX - 1)

    def along_y(step):
        return dp_at(step, core), seq

    def along_z(step):
        return dp, seq_at(0, step)

    sibling = (y * 2 + 1 - core, seq)

    def along_x(step):
        return dp, seq_at(step, 0)

    def part(c, half):
        return pl.ds(c * R, R) if half is None else pl.ds(c * R + half * H, H)

    token_ring = [
        Ring(T_PLAN, lambda s, half, c=c: tok.at[0, s, part(c, half)], ysend.at[c], yrecv.at[c], along_y)
        for c in range(NC)
    ]
    token_pair = [
        Pair(lambda s, c=c: tok.at[0, s, part(c, None)], lambda s, c=c: tok.at[1, s, part(c, None)],
             bsend.at[c], brecv.at[c], sibling)
        for c in range(NC)
    ]
    kv_ring = [
        Ring(KV_PLAN, lambda s, half, c=c: kv.at[s, part(c, half)], zsend.at[c], zrecv.at[c], along_z)
        for c in range(NC)
    ]
    att_ring = [
        Ring(ATT_PLAN, lambda s, half, c=c: att.at[0, s, part(c, half)], asend.at[c], arecv.at[c], along_y)
        for c in range(NC)
    ]
    att_pair = [
        Pair(lambda s, c=c: att.at[0, s, part(c, None)], lambda s, c=c: att.at[1, s, part(c, None)],
             csend.at[c], crecv.at[c], sibling)
        for c in range(NC)
    ]

    def weight_part(s, half):
        return wb.at[s] if half is None else wb.at[s, pl.ds(half * (NZ // 2), NZ // 2)]

    weight_ring = ShortRing(CROSS, weight_part, wcs, wcr, along_x)

    turn = lax.rem(x - dp + HEADS, NX)

    def out_tile(d):
        return wout.at[0, pl.ds(pl.multiple_of(z * 16, 16), 16), pl.ds(pl.multiple_of(d * FEAT, FEAT), FEAT)]

    def first_hop(i):
        d = NX * i + turn
        return remote(out_tile(d), wb.at[0, z, dp // NX], was.at[i], war.at[dp // NX], d, seq)

    own_tile = pltpu.make_async_copy(out_tile(dp), wb.at[0, z, dp // NX], local.at[6])

    def second_hop(k):
        return remote(wb.at[0, z], wb.at[0, z], wbs.at[k], wbr.at[k], dp, seq_at(0, k))


    def start_first():
        for i in range(HEADS // NX):
            @pl.when(NX * i + turn != dp)
            def _():
                first_hop(i).start()

            @pl.when(NX * i + turn == dp)
            def _():
                own_tile.start()

    def finish_first():
        for i in range(HEADS // NX):
            @pl.when(NX * i + turn != dp)
            def _():
                remote(out_tile(dp), wb.at[0, z, i], was.at[i], war.at[i], NX * i + turn, seq).wait_recv()

            @pl.when(NX * i + turn == dp)
            def _():
                own_tile.wait()

    def start_second():
        finish_first()

        @pl.loop(1, NZ)
        def _(k):
            second_hop(k).start()

    def start_third():
        @pl.loop(1, NZ)
        def _(k):
            second_hop(k).wait_recv()

        weight_ring.go(0)

    def project(o, s, c):
        rows = pl.ds(c * R, R)
        f = dp_at(-s, core if o == 0 else 1 - core)
        values = tok[o, s, rows, :].astype(F32)
        squares = values * values
        squares = squares[:, :HD] + squares[:, HD:]
        gains = jnp.concatenate([gain32[pl.ds(2 * f, 1), :], gain32[pl.ds(2 * f + 1, 1), :]], axis=1)
        scaled = (values * gains).astype(BF16)
        product = jnp.dot(
            scaled, w[pl.ds(pl.multiple_of(f * FEAT, FEAT), FEAT), :], preferred_element_type=F32
        )
        if (o, s) == (0, 0):
            ssq[rows, :] = squares
            acc[rows, :] = product
        else:
            ssq[rows, :] += squares
            acc[rows, :] += product

    q_copies = {}

    def projected(c):
        rows = pl.ds(c * R, R)
        total = jnp.sum(ssq[rows, :], axis=1, keepdims=True)
        inv_rms = lax.rsqrt(total / D + 1e-05)
        kv[0, rows, :] = (acc[rows, HD:] * inv_rms).astype(BF16)
        kv_ring[c].go(0)
        q[0, rows, :] = (acc[rows, :HD] * inv_rms).astype(BF16)
        for k in (2, 1, 3):
            copy = remote(q.at[0, rows], q.at[k, rows], qsend.at[c, k], qrecv.at[c, k], dp, seq_at(k, 0))
            copy.start()
            q_copies[c, k] = copy

    def attend(places, rows, s, c):
        keys = pl.ds(c * R, R)
        queries = q[places, rows, :]
        shape = queries.shape
        scores = lax.dot_general(
            queries.reshape(-1, HD), kv[s, keys, :HD], (((1,), (1,)), ((), ())), preferred_element_type=F32
        )
        same = segq[places, rows, :].reshape(-1, HD) == segk[s, 0:1, keys]
        weights = jnp.where(same, jnp.exp2(scores * SCALE), 0.0)
        product = jnp.dot(weights.astype(BF16), kv[s, keys, HD:], preferred_element_type=F32)
        if (s, c) == (0, 0):
            numer[places, rows, :] = product.reshape(shape)
            den[places, rows, :] = weights.reshape(shape)
        else:
            numer[places, rows, :] += product.reshape(shape)
            den[places, rows, :] += weights.reshape(shape)

    def tokens_in(c, slots):
        for t in slots:
            token_ring[c].arrived(t)
            token_ring[c].go(t)
            token_pair[c].go(t)

    def project_mine(c, slots):
        for t in slots:
            project(0, t, c)

    def project_theirs(c, slots):
        for t in slots:
            token_pair[c].arrived(t)
            project(1, t, c)

    def keys_in(c, slots):
        for t in slots:
            kv_ring[c].arrived(t)
            kv_ring[c].go(t)

    def queries_in(c):
        for k in range(1, NX):
            q_copies[c, k].wait_recv()

    def attend_all(chunks, slots, c):
        for t in slots:
            for qc in chunks:
                attend(slice(None), pl.ds(qc * R, R), t, c)

    def mix(o, s, c):
        rows = pl.ds(c * R, R)
        h = dp_at(-s, core if o == 0 else 1 - core)
        weight = wb[lax.rem(x - h - dp + 2 * HEADS, NX), :, h // NX].reshape(HD, FEAT)
        product = jnp.dot(att[o, s, rows, :], weight, preferred_element_type=F32)
        if (o, s) == (0, 0):
            acc[rows, :FEAT] = product
        else:
            acc[rows, :FEAT] += product

    def segments():
        loads[3].wait()
        gain32[...] = gainin[...].astype(F32)
        loads[4].wait()
        lane = lax.broadcasted_iota(jnp.int32, (HD, HD), 1)
        row = lax.broadcasted_iota(jnp.int32, (HD, HD), 0)
        lens_lane = jnp.concatenate([lenin[...].astype(F32), jnp.zeros((1, HD - DOCS), F32)], axis=1)
        lens_lane = jnp.broadcast_to(lens_lane, (HD, HD))
        lens_row = jnp.transpose(lens_lane)
        ends_lane = jnp.sum(jnp.where(row <= lane, lens_row, 0.0), axis=0, keepdims=True)
        ends_row = jnp.sum(jnp.where(lane <= row, lens_lane, 0.0), axis=1, keepdims=True)
        for s in range(NX):
            base = seq_at(-s, 0) * ROWS
            position = (lax.broadcasted_iota(jnp.int32, (ROWS, HD), 0) + base).astype(F32)
            count = jnp.sum(jnp.where(position >= ends_lane, 1.0, 0.0), axis=1, keepdims=True)
            segq[s] = jnp.broadcast_to(count, (ROWS, HD))
        for s in range(NZ):
            base = seq_at(0, -s) * ROWS
            position = (lax.broadcasted_iota(jnp.int32, (HD, ROWS), 1) + base).astype(F32)
            count = jnp.sum(jnp.where(position >= ends_row, 1.0, 0.0), axis=0, keepdims=True)
            segk[s] = jnp.broadcast_to(count, (8, ROWS))


    r_copies = {}

    def send_sums(k, c):
        rows = pl.ds(c * R, R)
        redo[k, c, :R, :] = numer[k, rows, :].astype(BF16)
        left = jnp.sum(jnp.transpose(den[k, rows, :]), axis=0, keepdims=True)
        at = lax.broadcasted_iota(jnp.int32, (16, HD), 0)
        terms = jnp.zeros((16, HD), F32)
        for i in range(3):
            term = left.astype(BF16).astype(F32)
            terms = jnp.where(at == i, term, terms)
            left = left - term
        redo[k, c, R:, :] = terms.astype(BF16)
        copy = remote(redo.at[k, c], redi.at[k, c], rsend.at[c, k], rrecv.at[c, k], dp, seq_at(-k, 0))
        copy.start()
        r_copies[c, k] = copy

    def combine(c):
        rows = pl.ds(c * R, R)
        down = jnp.sum(jnp.transpose(den[0, rows, :]), axis=0, keepdims=True)
        top = numer[0, rows, :]
        for k in (1, 3, 2):
            r_copies[c, k].wait_recv()
            top = top + redi[k, c, :R, :].astype(F32)
            terms = redi[k, c, R:, :].astype(F32)
            down = down + (terms[0:1, :] + terms[1:2, :] + terms[2:3, :])
        down = jnp.transpose(jnp.broadcast_to(down, (HD, HD)))
        att[0, 0, rows, :] = (top / down).astype(BF16)
        att_ring[c].go(0)
        att_pair[c].go(0)

    def run():
        start_first()
        token_ring[0].go(0)
        token_ring[1].go(0, only=2)
        for c in range(NC):
            token_pair[c].go(0)
        segments()
        loads[5].wait()
        project_mine(0, (0,))
        project_theirs(0, (0,))
        tokens_in(0, (2, 6))
        token_ring[1].go(0, only=1)
        tokens_in(0, (1, 7))
        start_second()
        project_mine(0, (2, 6, 1, 7))
        project_theirs(0, (2, 6, 1, 7))
        tokens_in(1, (2, 6))
        tokens_in(0, (3, 5))
        project_mine(0, (3, 5))
        tokens_in(0, (4,))
        project_mine(0, (4,))
        project_theirs(0, (3, 5, 4))
        projected(0)
        tokens_in(1, (1, 7))
        project_mine(1, (0, 2, 6, 1, 7))
        project_theirs(1, (0, 2, 6, 1, 7))
        tokens_in(1, (3, 5))
        project_mine(1, (3, 5))
        tokens_in(1, (4,))
        project_mine(1, (4,))
        project_theirs(1, (3, 5, 4))
        projected(1)
        start_third()
        keys_in(0, (2, 6))
        queries_in(0)
        attend_all((0,), (0,), 0)
        keys_in(0, (1, 7))
        attend_all((0,), (2, 6, 1, 7), 0)
        keys_in(0, (3, 5))
        attend_all((0,), (3, 5), 0)
        keys_in(1, (2, 6))
        queries_in(1)
        attend_all((1,), (0, 2, 6, 1, 7, 3, 5), 0)
        attend_all((0, 1), (0,), 1)
        keys_in(0, (4,))
        attend_all((0, 1), (4,), 0)
        keys_in(1, (1, 7))
        attend_all((0, 1), (2, 6, 1, 7), 1)
        for k in (1, 3):
            weight_ring.arrived(k)
            weight_ring.go(k)
        for group in (*token_ring, *token_pair):
            group.finish()
        keys_in(1, (3, 5))
        attend_all((0, 1), (3, 5), 1)
        keys_in(1, (4,))
        for c in range(NC):
            for k in (2, 1, 3):
                attend(k, pl.ds(c * R, R), 4, 1)
                send_sums(k, c)
        attend(0, pl.ds(0, ROWS), 4, 1)
        for group in kv_ring:
            group.finish()
        for copy in q_copies.values():
            copy.wait_send()
        for c in range(NC):
            combine(c)
        weight_ring.arrived(2)

        def att_in(slots):
            for c in range(NC):
                for t in slots:
                    att_ring[c].arrived(t)
                    att_ring[c].go(t)
                    att_pair[c].go(t)

        def mix_mine(slots):
            for c in range(NC):
                for t in slots:
                    mix(0, t, c)

        def mix_theirs(slots):
            for c in range(NC):
                for t in slots:
                    att_pair[c].arrived(t)
                    mix(1, t, c)

        mix_mine((0,))
        att_in((2, 6))
        mix_theirs((0,))
        att_in((1, 7))
        mix_mine((2, 6, 1, 7))
        mix_theirs((2, 6, 1, 7))
        att_in((3, 5))
        mix_mine((3, 5))
        att_in((4,))
        mix_mine((4,))
        mix_theirs((3, 5, 4))
        out[...] = acc[:, :FEAT].astype(BF16)

    run()
    for group in (*att_ring, *att_pair, weight_ring):
        group.finish()
    for copy in r_copies.values():
        copy.wait_send()

    for i in range(HEADS // NX):
        @pl.when(NX * i + turn != dp)
        def _():
            first_hop(i).wait_send()

    @pl.loop(1, NZ)
    def _(k):
        second_hop(k).wait_send()


def body(tokens, mask_flags, doc_lengths, mask_embed, norm_gain, qkv_weight, out_weight):
    vmem = pl.BlockSpec(memory_space=pltpu.VMEM)
    hbm = pl.BlockSpec(memory_space=pltpu.HBM)
    dma = lambda *shape: pltpu.SemaphoreType.DMA(shape)
    return pl.pallas_call(
        kernel,
        out_shape=jax.ShapeDtypeStruct((ROWS, FEAT), BF16),
        in_specs=[hbm] * 7,
        out_specs=vmem,
        scratch_shapes=[
            pltpu.VMEM((ROWS, FEAT), BF16),
            pltpu.VMEM((ROWS // HD, HD), jnp.int32),
            pltpu.VMEM((1, DOCS), jnp.int32),
            pltpu.VMEM((2, HD), BF16),
            pltpu.VMEM((D // HD, HD), BF16),
            pltpu.VMEM((D // HD, HD), F32),
            pltpu.VMEM((2, NY, ROWS, FEAT), BF16),
            pltpu.VMEM((D, 3 * HD), BF16),
            pltpu.VMEM((NZ, ROWS, 2 * HD), BF16),
            pltpu.VMEM((NX, ROWS, HD), BF16),
            pltpu.VMEM((NX, ROWS, HD), F32),
            pltpu.VMEM((NX, ROWS, HD), F32),
            pltpu.VMEM((NX, NC, R + 16, HD), BF16),
            pltpu.VMEM((NX, NC, R + 16, HD), BF16),
            pltpu.VMEM((2, NY, ROWS, HD), BF16),
            pltpu.VMEM((NX, NZ, HEADS // NX, 16, FEAT), BF16),
            pltpu.VMEM((ROWS, 3 * HD), F32),
            pltpu.VMEM((ROWS, HD), F32),
            pltpu.VMEM((NX, ROWS, HD), F32),
            pltpu.VMEM((NZ, 8, ROWS), F32),
            dma(7),
            dma(NC, 9), dma(NC, 9), dma(NC, 8), dma(NC, 8),
            dma(NC, 9), dma(NC, 9), dma(NC, NX), dma(NC, NX),
            dma(NC, NX), dma(NC, NX),
            dma(NC, 9), dma(NC, 9), dma(NC, 8), dma(NC, 8),
            dma(HEADS // NX), dma(HEADS // NX), dma(NZ), dma(NZ), dma(NX + 1), dma(NX + 1),
        ],
        compiler_params=pltpu.CompilerParams(
            collective_id=0, has_side_effects=True, vmem_limit_bytes=VMEM_BYTES
        ),
        name="attention_layer",
    )(
        tokens, mask_flags.reshape(ROWS // HD, HD), doc_lengths.reshape(1, DOCS), mask_embed.reshape(2, HD),
        norm_gain.reshape(D // HD, HD), qkv_weight.reshape(D, 3 * HD), out_weight,
    )


def solution(mesh):
    placed = (P("seq", "dp"), P("seq"), P(), P("dp"), P(), P(None, "dp", None), P("dp", None, None))
    return jax.shard_map(
        body, mesh=mesh, in_specs=placed, out_specs=P("seq", "dp"), check_vma=False
    )
```

```python
import math

import jax
import jax.numpy as jnp
from jax import lax
from jax.experimental import pallas as pl
from jax.experimental.pallas import tpu as pltpu
from jax.sharding import PartitionSpec as P

NY, NX, NZ = 8, 4, 8
ROWS, FEAT, HD, HEADS, D, DOCS = 256, 256, 128, 16, 4096, 64
VMEM_BYTES = 63 * 1024 * 1024
NC = 2
R = ROWS // NC
H = R // 2
F32, BF16 = jnp.float32, jnp.bfloat16
SCALE = math.log2(math.e) / math.sqrt(HD)


def remote(src, dst, send, recv, dp, seq):
    return pltpu.make_async_remote_copy(
        src_ref=src, dst_ref=dst, send_sem=send, recv_sem=recv,
        device_id=(dp, seq), device_id_type=pl.DeviceIdType.MESH,
    )


CROSS = ((0, 1), (0, -1), (1, 1), (3, -1))
TREE = ((0, 2), (0, -2), (0, 1), (0, -1), (2, 1), (6, -1), (2, 2), (6, -2))


class Ring:
    size = 8

    def __init__(self, plan, slot, send, recv, place):
        self.plan, self.slot, self.send, self.recv, self.place = plan, slot, send, recv, place
        self.copies = {}

    def go(self, s, only=None):
        for source, step in self.plan:
            if source == s and (only is None or abs(step) == only):
                to = (s + step) % self.size
                half = None if to != self.size // 2 else (0 if step > 0 else 1)
                sem = self.size if half == 1 else to
                copy = remote(
                    self.slot(s, half), self.slot(to, half), self.send.at[sem], self.recv.at[sem],
                    *self.place(step),
                )
                copy.start()
                self.copies[sem] = copy

    def arrived(self, s):
        for sem in (s, self.size) if s == self.size // 2 else (s,):
            self.copies[sem].wait_recv()

    def finish(self):
        for sem, copy in self.copies.items():
            copy.wait_send()


class ShortRing(Ring):
    size = 4


class Pair:
    def __init__(self, mine, theirs, send, recv, other):
        self.mine, self.theirs, self.send, self.recv, self.other = mine, theirs, send, recv, other
        self.copies = {}

    def go(self, s):
        copy = remote(self.mine(s), self.theirs(s), self.send.at[s], self.recv.at[s], *self.other)
        copy.start()
        self.copies[s] = copy

    def arrived(self, s):
        self.copies[s].wait_recv()

    def finish(self):
        for sem, copy in self.copies.items():
            copy.wait_send()


def kernel(
    tokens, flags, lens, embed, gain, wqkv, wout, out,
    tokin, flagin, lenin, embedin, gainin, gain32, tok, w, kv, q, numer, den, redo, redi, att, wb, acc, ssq, segq, segk,
    local, ysend, yrecv, bsend, brecv, zsend, zrecv, qsend, qrecv, rsend, rrecv,
    asend, arecv, csend, crecv, was, war, wbs, wbr, wcs, wcr,
):
    dp, seq = lax.axis_index("dp"), lax.axis_index("seq")
    y, core = dp // 2, lax.rem(dp, 2)
    x, z = seq // NZ, lax.rem(seq, NZ)

    loads = [
        pltpu.make_async_copy(there, here, local.at[i])
        for i, (there, here) in enumerate(
            [(tokens, tokin), (flags, flagin), (embed, embedin), (gain, gainin), (lens, lenin), (wqkv, w)]
        )
    ]
    for load in loads:
        load.start()

    def dp_at(dy, c):
        return lax.rem(y + dy + NY, NY) * 2 + c

    def seq_at(dx, dz):
        return lax.rem(x + dx + NX, NX) * NZ + lax.rem(z + dz + NZ, NZ)

    barrier = pltpu.get_barrier_semaphore()

    @pl.loop(1, HEADS)
    def _(k):
        pl.semaphore_signal(
            barrier, inc=1, device_id=(lax.rem(dp + k, HEADS), seq), device_id_type=pl.DeviceIdType.MESH
        )

    @pl.loop(1, NZ)
    def _(k):
        pl.semaphore_signal(barrier, inc=1, device_id=(dp, seq_at(0, k)), device_id_type=pl.DeviceIdType.MESH)

    @pl.loop(1, NX)
    def _(k):
        pl.semaphore_signal(barrier, inc=1, device_id=(dp, seq_at(k, 0)), device_id_type=pl.DeviceIdType.MESH)

    for load in loads[:3]:
        load.wait()
    embed_row = jnp.concatenate([embedin[0:1, :], embedin[1:2, :]], axis=1).astype(F32)
    for c in range(ROWS // HD):
        rows = pl.ds(c * HD, HD)
        flag = jnp.transpose(jnp.broadcast_to(flagin[c : c + 1, :].astype(F32), (HD, HD)))
        flag = jnp.concatenate([flag, flag], axis=1)
        masked = jnp.where(flag == 1.0, embed_row, tokin[rows, :].astype(F32))
        tok[0, 0, rows, :] = masked.astype(BF16)

    pl.semaphore_wait(barrier, HEADS - 1 + NZ - 1 + NX - 1)

    def along_y(step):
        return dp_at(step, core), seq

    def along_z(step):
        return dp, seq_at(0, step)

    sibling = (y * 2 + 1 - core, seq)

    def along_x(step):
        return dp, seq_at(step, 0)

    def part(c, half):
        return pl.ds(c * R, R) if half is None else pl.ds(c * R + half * H, H)

    token_ring = [
        Ring(TREE, lambda s, half, c=c: tok.at[0, s, part(c, half)], ysend.at[c], yrecv.at[c], along_y)
        for c in range(NC)
    ]
    token_pair = [
        Pair(lambda s, c=c: tok.at[0, s, part(c, None)], lambda s, c=c: tok.at[1, s, part(c, None)],
             bsend.at[c], brecv.at[c], sibling)
        for c in range(NC)
    ]
    kv_ring = [
        Ring(TREE, lambda s, half, c=c: kv.at[s, part(c, half)], zsend.at[c], zrecv.at[c], along_z)
        for c in range(NC)
    ]
    att_ring = [
        Ring(TREE, lambda s, half, c=c: att.at[0, s, part(c, half)], asend.at[c], arecv.at[c], along_y)
        for c in range(NC)
    ]
    att_pair = [
        Pair(lambda s, c=c: att.at[0, s, part(c, None)], lambda s, c=c: att.at[1, s, part(c, None)],
             csend.at[c], crecv.at[c], sibling)
        for c in range(NC)
    ]

    def weight_part(s, half):
        return wb.at[s] if half is None else wb.at[s, pl.ds(half * (NZ // 2), NZ // 2)]

    weight_ring = ShortRing(CROSS, weight_part, wcs, wcr, along_x)

    turn = lax.rem(x - dp + HEADS, NX)

    def out_tile(d):
        return wout.at[0, pl.ds(pl.multiple_of(z * 16, 16), 16), pl.ds(pl.multiple_of(d * FEAT, FEAT), FEAT)]

    def first_hop(i):
        d = NX * i + turn
        return remote(out_tile(d), wb.at[0, z, dp // NX], was.at[i], war.at[dp // NX], d, seq)

    own_tile = pltpu.make_async_copy(out_tile(dp), wb.at[0, z, dp // NX], local.at[6])

    def second_hop(k):
        return remote(wb.at[0, z], wb.at[0, z], wbs.at[k], wbr.at[k], dp, seq_at(0, k))


    def start_first():
        for i in range(HEADS // NX):
            @pl.when(NX * i + turn != dp)
            def _():
                first_hop(i).start()

            @pl.when(NX * i + turn == dp)
            def _():
                own_tile.start()

    def finish_first():
        for i in range(HEADS // NX):
            @pl.when(NX * i + turn != dp)
            def _():
                remote(out_tile(dp), wb.at[0, z, i], was.at[i], war.at[i], NX * i + turn, seq).wait_recv()

            @pl.when(NX * i + turn == dp)
            def _():
                own_tile.wait()

    def start_second():
        finish_first()

        @pl.loop(1, NZ)
        def _(k):
            second_hop(k).start()

    def finish_hops():
        for i in range(HEADS // NX):
            @pl.when(NX * i + turn != dp)
            def _():
                first_hop(i).wait_send()

        @pl.loop(1, NZ)
        def _(k):
            second_hop(k).wait_send()

    def start_third():
        @pl.loop(1, NZ)
        def _(k):
            second_hop(k).wait_recv()

        weight_ring.go(0)

    def project(o, s, c):
        rows = pl.ds(c * R, R)
        f = dp_at(-s, core if o == 0 else 1 - core)
        values = tok[o, s, rows, :].astype(F32)
        squares = values * values
        squares = squares[:, :HD] + squares[:, HD:]
        gains = jnp.concatenate([gain32[pl.ds(2 * f, 1), :], gain32[pl.ds(2 * f + 1, 1), :]], axis=1)
        scaled = (values * gains).astype(BF16)
        product = jnp.dot(
            scaled, w[pl.ds(pl.multiple_of(f * FEAT, FEAT), FEAT), :], preferred_element_type=F32
        )
        if (o, s) == (0, 0):
            ssq[rows, :] = squares
            acc[rows, :] = product
        else:
            ssq[rows, :] += squares
            acc[rows, :] += product

    q_copies = {}

    def projected(c):
        rows = pl.ds(c * R, R)
        total = jnp.sum(ssq[rows, :], axis=1, keepdims=True)
        inv_rms = lax.rsqrt(total / D + 1e-05)
        kv[0, rows, :] = (acc[rows, HD:] * inv_rms).astype(BF16)
        kv_ring[c].go(0)
        q[0, rows, :] = (acc[rows, :HD] * inv_rms).astype(BF16)
        for k in (2, 1, 3):
            copy = remote(q.at[0, rows], q.at[k, rows], qsend.at[c, k], qrecv.at[c, k], dp, seq_at(k, 0))
            copy.start()
            q_copies[c, k] = copy

    def attend(places, rows, s, c):
        keys = pl.ds(c * R, R)
        queries = q[places, rows, :]
        shape = queries.shape
        scores = lax.dot_general(
            queries.reshape(-1, HD), kv[s, keys, :HD], (((1,), (1,)), ((), ())), preferred_element_type=F32
        )
        same = segq[places, rows, :].reshape(-1, HD) == segk[s, 0:1, keys]
        weights = jnp.where(same, jnp.exp2(scores * SCALE), 0.0)
        product = jnp.dot(weights.astype(BF16), kv[s, keys, HD:], preferred_element_type=F32)
        if (s, c) == (0, 0):
            numer[places, rows, :] = product.reshape(shape)
            den[places, rows, :] = weights.reshape(shape)
        else:
            numer[places, rows, :] += product.reshape(shape)
            den[places, rows, :] += weights.reshape(shape)

    def tokens_in(c, slots):
        for t in slots:
            token_ring[c].arrived(t)
            token_ring[c].go(t)
            token_pair[c].go(t)

    def project_mine(c, slots):
        for t in slots:
            project(0, t, c)

    def project_theirs(c, slots):
        for t in slots:
            token_pair[c].arrived(t)
            project(1, t, c)

    def keys_in(c, slots):
        for t in slots:
            kv_ring[c].arrived(t)
            kv_ring[c].go(t)

    def queries_in(c):
        for k in range(1, NX):
            q_copies[c, k].wait_recv()

    def attend_all(chunks, slots, c):
        for t in slots:
            for qc in chunks:
                attend(slice(None), pl.ds(qc * R, R), t, c)

    def mix(o, s, c):
        rows = pl.ds(c * R, R)
        h = dp_at(-s, core if o == 0 else 1 - core)
        weight = wb[lax.rem(x - h - dp + 2 * HEADS, NX), :, h // NX].reshape(HD, FEAT)
        product = jnp.dot(att[o, s, rows, :], weight, preferred_element_type=F32)
        if (o, s) == (0, 0):
            acc[rows, :FEAT] = product
        else:
            acc[rows, :FEAT] += product

    def segments():
        loads[3].wait()
        gain32[...] = gainin[...].astype(F32)
        loads[4].wait()
        lane = lax.broadcasted_iota(jnp.int32, (HD, HD), 1)
        row = lax.broadcasted_iota(jnp.int32, (HD, HD), 0)
        lens_lane = jnp.concatenate([lenin[...].astype(F32), jnp.zeros((1, HD - DOCS), F32)], axis=1)
        lens_lane = jnp.broadcast_to(lens_lane, (HD, HD))
        lens_row = jnp.transpose(lens_lane)
        ends_lane = jnp.sum(jnp.where(row <= lane, lens_row, 0.0), axis=0, keepdims=True)
        ends_row = jnp.sum(jnp.where(lane <= row, lens_lane, 0.0), axis=1, keepdims=True)
        for s in range(NX):
            base = seq_at(-s, 0) * ROWS
            position = (lax.broadcasted_iota(jnp.int32, (ROWS, HD), 0) + base).astype(F32)
            count = jnp.sum(jnp.where(position >= ends_lane, 1.0, 0.0), axis=1, keepdims=True)
            segq[s] = jnp.broadcast_to(count, (ROWS, HD))
        for s in range(NZ):
            base = seq_at(0, -s) * ROWS
            position = (lax.broadcasted_iota(jnp.int32, (HD, ROWS), 1) + base).astype(F32)
            count = jnp.sum(jnp.where(position >= ends_row, 1.0, 0.0), axis=0, keepdims=True)
            segk[s] = jnp.broadcast_to(count, (8, ROWS))


    r_copies = {}

    def send_sums(k, c):
        rows = pl.ds(c * R, R)
        redo[k, c, :R, :] = numer[k, rows, :].astype(BF16)
        left = jnp.sum(jnp.transpose(den[k, rows, :]), axis=0, keepdims=True)
        at = lax.broadcasted_iota(jnp.int32, (16, HD), 0)
        terms = jnp.zeros((16, HD), F32)
        for i in range(3):
            term = left.astype(BF16).astype(F32)
            terms = jnp.where(at == i, term, terms)
            left = left - term
        redo[k, c, R:, :] = terms.astype(BF16)
        copy = remote(redo.at[k, c], redi.at[k, c], rsend.at[c, k], rrecv.at[c, k], dp, seq_at(-k, 0))
        copy.start()
        r_copies[c, k] = copy

    def combine(c):
        rows = pl.ds(c * R, R)
        down = jnp.sum(jnp.transpose(den[0, rows, :]), axis=0, keepdims=True)
        top = numer[0, rows, :]
        for k in (1, 3, 2):
            r_copies[c, k].wait_recv()
            top = top + redi[k, c, :R, :].astype(F32)
            terms = redi[k, c, R:, :].astype(F32)
            down = down + (terms[0:1, :] + terms[1:2, :] + terms[2:3, :])
        down = jnp.transpose(jnp.broadcast_to(down, (HD, HD)))
        att[0, 0, rows, :] = (top / down).astype(BF16)
        att_ring[c].go(0)
        att_pair[c].go(0)

    def run():
        start_first()
        token_ring[0].go(0)
        token_ring[1].go(0, only=2)
        for c in range(NC):
            token_pair[c].go(0)
        segments()
        loads[5].wait()
        project_mine(0, (0,))
        project_theirs(0, (0,))
        tokens_in(0, (2, 6))
        token_ring[1].go(0, only=1)
        tokens_in(0, (1, 7))
        start_second()
        project_mine(0, (2, 6, 1, 7))
        project_theirs(0, (2, 6, 1, 7))
        tokens_in(1, (2, 6))
        tokens_in(0, (3, 5))
        project_mine(0, (3, 5))
        tokens_in(0, (4,))
        project_mine(0, (4,))
        project_theirs(0, (3, 5, 4))
        projected(0)
        tokens_in(1, (1, 7))
        project_mine(1, (0, 2, 6, 1, 7))
        project_theirs(1, (0, 2, 6, 1, 7))
        tokens_in(1, (3, 5))
        project_mine(1, (3, 5))
        tokens_in(1, (4,))
        project_mine(1, (4,))
        project_theirs(1, (3, 5, 4))
        projected(1)
        start_third()
        keys_in(0, (2, 6))
        queries_in(0)
        attend_all((0,), (0,), 0)
        keys_in(0, (1, 7))
        attend_all((0,), (2, 6, 1, 7), 0)
        keys_in(1, (2, 6))
        keys_in(0, (3, 5))
        attend_all((0,), (3, 5), 0)
        queries_in(1)
        attend_all((1,), (0, 2, 6, 1, 7, 3, 5), 0)
        attend_all((0, 1), (0,), 1)
        keys_in(0, (4,))
        attend_all((0, 1), (4,), 0)
        keys_in(1, (1, 7))
        attend_all((0, 1), (2, 6, 1, 7), 1)
        for k in (1, 3):
            weight_ring.arrived(k)
            weight_ring.go(k)
        for group in (*token_ring, *token_pair):
            group.finish()
        keys_in(1, (3, 5))
        attend_all((0, 1), (3, 5), 1)
        keys_in(1, (4,))
        for c in range(NC):
            for k in (2, 1, 3):
                attend(k, pl.ds(c * R, R), 4, 1)
                send_sums(k, c)
        attend(0, pl.ds(0, ROWS), 4, 1)
        for group in kv_ring:
            group.finish()
        for copy in q_copies.values():
            copy.wait_send()
        for c in range(NC):
            combine(c)
        weight_ring.arrived(2)

        def att_in(slots):
            for c in range(NC):
                for t in slots:
                    att_ring[c].arrived(t)
                    att_ring[c].go(t)
                    att_pair[c].go(t)

        def mix_mine(slots):
            for c in range(NC):
                for t in slots:
                    mix(0, t, c)

        def mix_theirs(slots):
            for c in range(NC):
                for t in slots:
                    att_pair[c].arrived(t)
                    mix(1, t, c)

        mix_mine((0,))
        for copy in r_copies.values():
            copy.wait_send()
        weight_ring.finish()
        finish_hops()
        att_in((2, 6))
        mix_theirs((0,))
        att_in((1, 7))
        mix_mine((2, 6, 1, 7))
        mix_theirs((2, 6, 1, 7))
        att_in((3, 5))
        mix_mine((3, 5))
        att_in((4,))
        mix_mine((4,))
        for group in att_ring:
            group.finish()
        mix_theirs((3, 5, 4))
        out[...] = acc[:, :FEAT].astype(BF16)

    run()
    for group in att_pair:
        group.finish()


def body(tokens, mask_flags, doc_lengths, mask_embed, norm_gain, qkv_weight, out_weight):
    vmem = pl.BlockSpec(memory_space=pltpu.VMEM)
    hbm = pl.BlockSpec(memory_space=pltpu.HBM)
    dma = lambda *shape: pltpu.SemaphoreType.DMA(shape)
    return pl.pallas_call(
        kernel,
        out_shape=jax.ShapeDtypeStruct((ROWS, FEAT), BF16),
        in_specs=[hbm] * 7,
        out_specs=vmem,
        scratch_shapes=[
            pltpu.VMEM((ROWS, FEAT), BF16),
            pltpu.VMEM((ROWS // HD, HD), jnp.int32),
            pltpu.VMEM((1, DOCS), jnp.int32),
            pltpu.VMEM((2, HD), BF16),
            pltpu.VMEM((D // HD, HD), BF16),
            pltpu.VMEM((D // HD, HD), F32),
            pltpu.VMEM((2, NY, ROWS, FEAT), BF16),
            pltpu.VMEM((D, 3 * HD), BF16),
            pltpu.VMEM((NZ, ROWS, 2 * HD), BF16),
            pltpu.VMEM((NX, ROWS, HD), BF16),
            pltpu.VMEM((NX, ROWS, HD), F32),
            pltpu.VMEM((NX, ROWS, HD), F32),
            pltpu.VMEM((NX, NC, R + 16, HD), BF16),
            pltpu.VMEM((NX, NC, R + 16, HD), BF16),
            pltpu.VMEM((2, NY, ROWS, HD), BF16),
            pltpu.VMEM((NX, NZ, HEADS // NX, 16, FEAT), BF16),
            pltpu.VMEM((ROWS, 3 * HD), F32),
            pltpu.VMEM((ROWS, HD), F32),
            pltpu.VMEM((NX, ROWS, HD), F32),
            pltpu.VMEM((NZ, 8, ROWS), F32),
            dma(7),
            dma(NC, 9), dma(NC, 9), dma(NC, 8), dma(NC, 8),
            dma(NC, 9), dma(NC, 9), dma(NC, NX), dma(NC, NX),
            dma(NC, NX), dma(NC, NX),
            dma(NC, 9), dma(NC, 9), dma(NC, 8), dma(NC, 8),
            dma(HEADS // NX), dma(HEADS // NX), dma(NZ), dma(NZ), dma(NX + 1), dma(NX + 1),
        ],
        compiler_params=pltpu.CompilerParams(
            collective_id=0, has_side_effects=True, vmem_limit_bytes=VMEM_BYTES
        ),
        name="attention_layer",
    )(
        tokens, mask_flags.reshape(ROWS // HD, HD), doc_lengths.reshape(1, DOCS), mask_embed.reshape(2, HD),
        norm_gain.reshape(D // HD, HD), qkv_weight.reshape(D, 3 * HD), out_weight,
    )


def solution(mesh):
    placed = (P("seq", "dp"), P("seq"), P(), P("dp"), P(), P(None, "dp", None), P("dp", None, None))
    return jax.shard_map(
        body, mesh=mesh, in_specs=placed, out_specs=P("seq", "dp"), check_vma=False
    )
```

```python
import math

import jax
import jax.numpy as jnp
from jax import lax
from jax.experimental import pallas as pl
from jax.experimental.pallas import tpu as pltpu
from jax.sharding import PartitionSpec as P

NY, NX, NZ = 8, 4, 8
ROWS, FEAT, HD, HEADS, D, DOCS = 256, 256, 128, 16, 4096, 64
VMEM_BYTES = 63 * 1024 * 1024
NC = 2
R = ROWS // NC
H = R // 2
F32, BF16 = jnp.float32, jnp.bfloat16
SCALE = math.log2(math.e) / math.sqrt(HD)


def remote(src, dst, send, recv, dp, seq):
    return pltpu.make_async_remote_copy(
        src_ref=src, dst_ref=dst, send_sem=send, recv_sem=recv,
        device_id=(dp, seq), device_id_type=pl.DeviceIdType.MESH,
    )


CROSS = ((0, 1), (0, -1), (1, 1), (3, -1))
TREE = ((0, 2), (0, -2), (0, 1), (0, -1), (2, 1), (6, -1), (2, 2), (6, -2))


class Ring:
    size = 8

    def __init__(self, plan, slot, send, recv, place):
        self.plan, self.slot, self.send, self.recv, self.place = plan, slot, send, recv, place
        self.copies = {}

    def go(self, s, only=None):
        for source, step in self.plan:
            if source == s and (only is None or abs(step) == only):
                to = (s + step) % self.size
                half = None if to != self.size // 2 else (0 if step > 0 else 1)
                sem = self.size if half == 1 else to
                copy = remote(
                    self.slot(s, half), self.slot(to, half), self.send.at[sem], self.recv.at[sem],
                    *self.place(step),
                )
                copy.start()
                self.copies[sem] = copy

    def arrived(self, s):
        for sem in (s, self.size) if s == self.size // 2 else (s,):
            self.copies[sem].wait_recv()

    def finish(self):
        for sem, copy in self.copies.items():
            copy.wait_send()


class ShortRing(Ring):
    size = 4


class Pair:
    def __init__(self, mine, theirs, send, recv, other):
        self.mine, self.theirs, self.send, self.recv, self.other = mine, theirs, send, recv, other
        self.copies = {}

    def go(self, s):
        copy = remote(self.mine(s), self.theirs(s), self.send.at[s], self.recv.at[s], *self.other)
        copy.start()
        self.copies[s] = copy

    def arrived(self, s):
        self.copies[s].wait_recv()

    def finish(self):
        for sem, copy in self.copies.items():
            copy.wait_send()


def kernel(
    tokens, flags, lens, embed, gain, wqkv, wout, out,
    tokin, flagin, lenin, embedin, gainin, gain32, tok, w, kv, q, numer, den, redo, redi, att, wb, acc, ssq, segq, segk,
    local, ysend, yrecv, bsend, brecv, zsend, zrecv, qsend, qrecv, rsend, rrecv,
    asend, arecv, csend, crecv, was, war, wbs, wbr, wcs, wcr,
):
    dp, seq = lax.axis_index("dp"), lax.axis_index("seq")
    y, core = dp // 2, lax.rem(dp, 2)
    x, z = seq // NZ, lax.rem(seq, NZ)

    loads = [
        pltpu.make_async_copy(there, here, local.at[i])
        for i, (there, here) in enumerate(
            [(tokens, tokin), (flags, flagin), (embed, embedin), (gain, gainin), (lens, lenin), (wqkv, w)]
        )
    ]

    def dp_at(dy, c):
        return lax.rem(y + dy + NY, NY) * 2 + c

    def seq_at(dx, dz):
        return lax.rem(x + dx + NX, NX) * NZ + lax.rem(z + dz + NZ, NZ)

    barrier = pltpu.get_barrier_semaphore()

    @pl.loop(1, HEADS)
    def _(k):
        pl.semaphore_signal(
            barrier, inc=1, device_id=(lax.rem(dp + k, HEADS), seq), device_id_type=pl.DeviceIdType.MESH
        )

    @pl.loop(1, NZ)
    def _(k):
        pl.semaphore_signal(barrier, inc=1, device_id=(dp, seq_at(0, k)), device_id_type=pl.DeviceIdType.MESH)

    @pl.loop(1, NX)
    def _(k):
        pl.semaphore_signal(barrier, inc=1, device_id=(dp, seq_at(k, 0)), device_id_type=pl.DeviceIdType.MESH)

    for load in loads:
        load.start()
    for load in loads[:3]:
        load.wait()
    embed_row = jnp.concatenate([embedin[0:1, :], embedin[1:2, :]], axis=1).astype(F32)
    for c in range(ROWS // HD):
        rows = pl.ds(c * HD, HD)
        flag = jnp.transpose(jnp.broadcast_to(flagin[c : c + 1, :].astype(F32), (HD, HD)))
        flag = jnp.concatenate([flag, flag], axis=1)
        masked = jnp.where(flag == 1.0, embed_row, tokin[rows, :].astype(F32))
        tok[0, 0, rows, :] = masked.astype(BF16)

    pl.semaphore_wait(barrier, HEADS - 1 + NZ - 1 + NX - 1)

    def along_y(step):
        return dp_at(step, core), seq

    def along_z(step):
        return dp, seq_at(0, step)

    sibling = (y * 2 + 1 - core, seq)

    def along_x(step):
        return dp, seq_at(step, 0)

    def part(c, half):
        return pl.ds(c * R, R) if half is None else pl.ds(c * R + half * H, H)

    token_ring = [
        Ring(TREE, lambda s, half, c=c: tok.at[0, s, part(c, half)], ysend.at[c], yrecv.at[c], along_y)
        for c in range(NC)
    ]
    token_pair = [
        Pair(lambda s, c=c: tok.at[0, s, part(c, None)], lambda s, c=c: tok.at[1, s, part(c, None)],
             bsend.at[c], brecv.at[c], sibling)
        for c in range(NC)
    ]
    kv_ring = [
        Ring(TREE, lambda s, half, c=c: kv.at[s, part(c, half)], zsend.at[c], zrecv.at[c], along_z)
        for c in range(NC)
    ]
    att_ring = [
        Ring(TREE, lambda s, half, c=c: att.at[0, s, part(c, half)], asend.at[c], arecv.at[c], along_y)
        for c in range(NC)
    ]
    att_pair = [
        Pair(lambda s, c=c: att.at[0, s, part(c, None)], lambda s, c=c: att.at[1, s, part(c, None)],
             csend.at[c], crecv.at[c], sibling)
        for c in range(NC)
    ]

    def weight_part(s, half):
        return wb.at[s] if half is None else wb.at[s, pl.ds(half * (NZ // 2), NZ // 2)]

    weight_ring = ShortRing(CROSS, weight_part, wcs, wcr, along_x)

    turn = lax.rem(x - dp + HEADS, NX)

    def out_tile(d):
        return wout.at[0, pl.ds(pl.multiple_of(z * 16, 16), 16), pl.ds(pl.multiple_of(d * FEAT, FEAT), FEAT)]

    def first_hop(i):
        d = NX * i + turn
        return remote(out_tile(d), wb.at[0, z, dp // NX], was.at[i], war.at[dp // NX], d, seq)

    own_tile = pltpu.make_async_copy(out_tile(dp), wb.at[0, z, dp // NX], local.at[6])

    def second_hop(k):
        return remote(wb.at[0, z], wb.at[0, z], wbs.at[k], wbr.at[k], dp, seq_at(0, k))


    def start_first():
        for i in range(HEADS // NX):
            @pl.when(NX * i + turn != dp)
            def _():
                first_hop(i).start()

            @pl.when(NX * i + turn == dp)
            def _():
                own_tile.start()

    def finish_first():
        for i in range(HEADS // NX):
            @pl.when(NX * i + turn != dp)
            def _():
                remote(out_tile(dp), wb.at[0, z, i], was.at[i], war.at[i], NX * i + turn, seq).wait_recv()

            @pl.when(NX * i + turn == dp)
            def _():
                own_tile.wait()

    def start_second():
        finish_first()

        @pl.loop(1, NZ)
        def _(k):
            second_hop(k).start()

    def finish_hops():
        for i in range(HEADS // NX):
            @pl.when(NX * i + turn != dp)
            def _():
                first_hop(i).wait_send()

        @pl.loop(1, NZ)
        def _(k):
            second_hop(k).wait_send()

    def start_third():
        @pl.loop(1, NZ)
        def _(k):
            second_hop(k).wait_recv()

        weight_ring.go(0)

    def project(o, s, c):
        rows = pl.ds(c * R, R)
        f = dp_at(-s, core if o == 0 else 1 - core)
        values = tok[o, s, rows, :].astype(F32)
        squares = values * values
        squares = squares[:, :HD] + squares[:, HD:]
        gains = jnp.concatenate([gain32[pl.ds(2 * f, 1), :], gain32[pl.ds(2 * f + 1, 1), :]], axis=1)
        scaled = (values * gains).astype(BF16)
        product = jnp.dot(
            scaled, w[pl.ds(pl.multiple_of(f * FEAT, FEAT), FEAT), :], preferred_element_type=F32
        )
        if (o, s) == (0, 0):
            ssq[rows, :] = squares
            acc[rows, :] = product
        else:
            ssq[rows, :] += squares
            acc[rows, :] += product

    q_copies = {}

    def projected(c):
        rows = pl.ds(c * R, R)
        total = jnp.sum(ssq[rows, :], axis=1, keepdims=True)
        inv_rms = lax.rsqrt(total / D + 1e-05)
        kv[0, rows, :] = (acc[rows, HD:] * inv_rms).astype(BF16)
        kv_ring[c].go(0)
        q[0, rows, :] = (acc[rows, :HD] * inv_rms).astype(BF16)
        for k in (2, 1, 3):
            copy = remote(q.at[0, rows], q.at[k, rows], qsend.at[c, k], qrecv.at[c, k], dp, seq_at(k, 0))
            copy.start()
            q_copies[c, k] = copy

    def attend(places, rows, s, c):
        keys = pl.ds(c * R, R)
        queries = q[places, rows, :]
        shape = queries.shape
        scores = lax.dot_general(
            queries.reshape(-1, HD), kv[s, keys, :HD], (((1,), (1,)), ((), ())), preferred_element_type=F32
        )
        same = segq[places, rows, :].reshape(-1, HD) == segk[s, 0:1, keys]
        weights = jnp.where(same, jnp.exp2(scores * SCALE), 0.0)
        product = jnp.dot(weights.astype(BF16), kv[s, keys, HD:], preferred_element_type=F32)
        if (s, c) == (0, 0):
            numer[places, rows, :] = product.reshape(shape)
            den[places, rows, :] = weights.reshape(shape)
        else:
            numer[places, rows, :] += product.reshape(shape)
            den[places, rows, :] += weights.reshape(shape)

    def tokens_in(c, slots):
        for t in slots:
            token_ring[c].arrived(t)
            token_ring[c].go(t)
            token_pair[c].go(t)

    def project_mine(c, slots):
        for t in slots:
            project(0, t, c)

    def project_theirs(c, slots):
        for t in slots:
            token_pair[c].arrived(t)
            project(1, t, c)

    def keys_in(c, slots):
        for t in slots:
            kv_ring[c].arrived(t)
            kv_ring[c].go(t)

    def queries_in(c):
        for k in range(1, NX):
            q_copies[c, k].wait_recv()

    def attend_all(chunks, slots, c):
        for t in slots:
            for qc in chunks:
                attend(slice(None), pl.ds(qc * R, R), t, c)

    def mix(o, s, c):
        rows = pl.ds(c * R, R)
        h = dp_at(-s, core if o == 0 else 1 - core)
        weight = wb[lax.rem(x - h - dp + 2 * HEADS, NX), :, h // NX].reshape(HD, FEAT)
        product = jnp.dot(att[o, s, rows, :], weight, preferred_element_type=F32)
        if (o, s) == (0, 0):
            acc[rows, :FEAT] = product
        else:
            acc[rows, :FEAT] += product

    def segments():
        loads[3].wait()
        gain32[...] = gainin[...].astype(F32)
        loads[4].wait()
        lane = lax.broadcasted_iota(jnp.int32, (HD, HD), 1)
        row = lax.broadcasted_iota(jnp.int32, (HD, HD), 0)
        lens_lane = jnp.concatenate([lenin[...].astype(F32), jnp.zeros((1, HD - DOCS), F32)], axis=1)
        lens_lane = jnp.broadcast_to(lens_lane, (HD, HD))
        lens_row = jnp.transpose(lens_lane)
        ends_lane = jnp.sum(jnp.where(row <= lane, lens_row, 0.0), axis=0, keepdims=True)
        ends_row = jnp.sum(jnp.where(lane <= row, lens_lane, 0.0), axis=1, keepdims=True)
        for s in range(NX):
            base = seq_at(-s, 0) * ROWS
            position = (lax.broadcasted_iota(jnp.int32, (ROWS, HD), 0) + base).astype(F32)
            count = jnp.sum(jnp.where(position >= ends_lane, 1.0, 0.0), axis=1, keepdims=True)
            segq[s] = jnp.broadcast_to(count, (ROWS, HD))
        for s in range(NZ):
            base = seq_at(0, -s) * ROWS
            position = (lax.broadcasted_iota(jnp.int32, (HD, ROWS), 1) + base).astype(F32)
            count = jnp.sum(jnp.where(position >= ends_row, 1.0, 0.0), axis=0, keepdims=True)
            segk[s] = jnp.broadcast_to(count, (8, ROWS))


    r_copies = {}

    def send_sums(k, c):
        rows = pl.ds(c * R, R)
        redo[k, c, :R, :] = numer[k, rows, :].astype(BF16)
        left = jnp.sum(jnp.transpose(den[k, rows, :]), axis=0, keepdims=True)
        at = lax.broadcasted_iota(jnp.int32, (16, HD), 0)
        terms = jnp.zeros((16, HD), F32)
        for i in range(3):
            term = left.astype(BF16).astype(F32)
            terms = jnp.where(at == i, term, terms)
            left = left - term
        redo[k, c, R:, :] = terms.astype(BF16)
        copy = remote(redo.at[k, c], redi.at[k, c], rsend.at[c, k], rrecv.at[c, k], dp, seq_at(-k, 0))
        copy.start()
        r_copies[c, k] = copy

    def combine(c):
        rows = pl.ds(c * R, R)
        down = jnp.sum(jnp.transpose(den[0, rows, :]), axis=0, keepdims=True)
        top = numer[0, rows, :]
        for k in (1, 3, 2):
            r_copies[c, k].wait_recv()
            top = top + redi[k, c, :R, :].astype(F32)
            terms = redi[k, c, R:, :].astype(F32)
            down = down + (terms[0:1, :] + terms[1:2, :] + terms[2:3, :])
        down = jnp.transpose(jnp.broadcast_to(down, (HD, HD)))
        att[0, 0, rows, :] = (top / down).astype(BF16)
        att_ring[c].go(0)
        att_pair[c].go(0)

    def run():
        start_first()
        token_ring[0].go(0)
        token_ring[1].go(0, only=2)
        for c in range(NC):
            token_pair[c].go(0)
        segments()
        loads[5].wait()
        project_mine(0, (0,))
        project_theirs(0, (0,))
        tokens_in(0, (2, 6))
        token_ring[1].go(0, only=1)
        tokens_in(0, (1, 7))
        start_second()
        project_mine(0, (2, 6, 1, 7))
        project_theirs(0, (2, 6, 1, 7))
        tokens_in(1, (2, 6))
        tokens_in(0, (3, 5))
        project_mine(0, (3, 5))
        tokens_in(0, (4,))
        project_mine(0, (4,))
        project_theirs(0, (3, 5, 4))
        projected(0)
        tokens_in(1, (1, 7))
        project_mine(1, (0, 2, 6, 1, 7))
        project_theirs(1, (0, 2, 6, 1, 7))
        tokens_in(1, (3, 5))
        project_mine(1, (3, 5))
        tokens_in(1, (4,))
        project_mine(1, (4,))
        project_theirs(1, (3, 5, 4))
        projected(1)
        start_third()
        keys_in(0, (2, 6))
        queries_in(0)
        attend_all((0,), (0,), 0)
        keys_in(0, (1, 7))
        attend_all((0,), (2, 6, 1, 7), 0)
        keys_in(1, (2, 6))
        keys_in(0, (3, 5))
        attend_all((0,), (3, 5), 0)
        queries_in(1)
        attend_all((1,), (0, 2, 6, 1, 7, 3, 5), 0)
        attend_all((0, 1), (0,), 1)
        keys_in(0, (4,))
        attend_all((0, 1), (4,), 0)
        keys_in(1, (1, 7))
        attend_all((0, 1), (2, 6, 1, 7), 1)
        for k in (1, 3):
            weight_ring.arrived(k)
            weight_ring.go(k)
        for group in (*token_ring, *token_pair):
            group.finish()
        keys_in(1, (3, 5))
        attend_all((0, 1), (3, 5), 1)
        keys_in(1, (4,))
        for c in range(NC):
            attend_all((c,), (4,), 1)
            for k in (2, 1, 3):
                send_sums(k, c)
        for group in kv_ring:
            group.finish()
        for copy in q_copies.values():
            copy.wait_send()
        for c in range(NC):
            combine(c)
        weight_ring.arrived(2)

        def att_in(slots):
            for c in range(NC):
                for t in slots:
                    att_ring[c].arrived(t)
                    att_ring[c].go(t)
                    att_pair[c].go(t)

        def mix_mine(slots):
            for c in range(NC):
                for t in slots:
                    mix(0, t, c)

        def mix_theirs(slots):
            for c in range(NC):
                for t in slots:
                    att_pair[c].arrived(t)
                    mix(1, t, c)

        mix_mine((0,))
        for copy in r_copies.values():
            copy.wait_send()
        weight_ring.finish()
        finish_hops()
        att_in((2, 6))
        mix_theirs((0,))
        att_in((1, 7))
        mix_mine((2, 6, 1, 7))
        mix_theirs((2, 6, 1, 7))
        att_in((3, 5))
        mix_mine((3, 5))
        att_in((4,))
        mix_mine((4,))
        for group in att_ring:
            group.finish()
        mix_theirs((3, 5, 4))
        out[...] = acc[:, :FEAT].astype(BF16)

    run()
    for group in att_pair:
        group.finish()


def body(tokens, mask_flags, doc_lengths, mask_embed, norm_gain, qkv_weight, out_weight):
    vmem = pl.BlockSpec(memory_space=pltpu.VMEM)
    hbm = pl.BlockSpec(memory_space=pltpu.HBM)
    dma = lambda *shape: pltpu.SemaphoreType.DMA(shape)
    return pl.pallas_call(
        kernel,
        out_shape=jax.ShapeDtypeStruct((ROWS, FEAT), BF16),
        in_specs=[hbm] * 7,
        out_specs=vmem,
        scratch_shapes=[
            pltpu.VMEM((ROWS, FEAT), BF16),
            pltpu.VMEM((ROWS // HD, HD), jnp.int32),
            pltpu.VMEM((1, DOCS), jnp.int32),
            pltpu.VMEM((2, HD), BF16),
            pltpu.VMEM((D // HD, HD), BF16),
            pltpu.VMEM((D // HD, HD), F32),
            pltpu.VMEM((2, NY, ROWS, FEAT), BF16),
            pltpu.VMEM((D, 3 * HD), BF16),
            pltpu.VMEM((NZ, ROWS, 2 * HD), BF16),
            pltpu.VMEM((NX, ROWS, HD), BF16),
            pltpu.VMEM((NX, ROWS, HD), F32),
            pltpu.VMEM((NX, ROWS, HD), F32),
            pltpu.VMEM((NX, NC, R + 16, HD), BF16),
            pltpu.VMEM((NX, NC, R + 16, HD), BF16),
            pltpu.VMEM((2, NY, ROWS, HD), BF16),
            pltpu.VMEM((NX, NZ, HEADS // NX, 16, FEAT), BF16),
            pltpu.VMEM((ROWS, 3 * HD), F32),
            pltpu.VMEM((ROWS, HD), F32),
            pltpu.VMEM((NX, ROWS, HD), F32),
            pltpu.VMEM((NZ, 8, ROWS), F32),
            dma(7),
            dma(NC, 9), dma(NC, 9), dma(NC, 8), dma(NC, 8),
            dma(NC, 9), dma(NC, 9), dma(NC, NX), dma(NC, NX),
            dma(NC, NX), dma(NC, NX),
            dma(NC, 9), dma(NC, 9), dma(NC, 8), dma(NC, 8),
            dma(HEADS // NX), dma(HEADS // NX), dma(NZ), dma(NZ), dma(NX + 1), dma(NX + 1),
        ],
        compiler_params=pltpu.CompilerParams(
            collective_id=0, has_side_effects=True, vmem_limit_bytes=VMEM_BYTES
        ),
        name="attention_layer",
    )(
        tokens, mask_flags.reshape(ROWS // HD, HD), doc_lengths.reshape(1, DOCS), mask_embed.reshape(2, HD),
        norm_gain.reshape(D // HD, HD), qkv_weight.reshape(D, 3 * HD), out_weight,
    )


def solution(mesh):
    placed = (P("seq", "dp"), P("seq"), P(), P("dp"), P(), P(None, "dp", None), P("dp", None, None))
    return jax.shard_map(
        body, mesh=mesh, in_specs=placed, out_specs=P("seq", "dp"), check_vma=False
    )
```

```python
import math

import jax
import jax.numpy as jnp
from jax import lax
from jax.experimental import pallas as pl
from jax.experimental.pallas import tpu as pltpu
from jax.sharding import PartitionSpec as P

NY, NX, NZ = 8, 4, 8
ROWS, FEAT, HD, HEADS, D, DOCS = 256, 256, 128, 16, 4096, 64
VMEM_BYTES = 63 * 1024 * 1024
NC = 2
R = ROWS // NC
H = R // 2
F32, BF16 = jnp.float32, jnp.bfloat16
SCALE = math.log2(math.e) / math.sqrt(HD)


def remote(src, dst, send, recv, dp, seq):
    return pltpu.make_async_remote_copy(
        src_ref=src, dst_ref=dst, send_sem=send, recv_sem=recv,
        device_id=(dp, seq), device_id_type=pl.DeviceIdType.MESH,
    )


CROSS = ((0, 1), (0, -1), (1, 1), (3, -1))
TREE = ((0, 2), (0, -2), (0, 1), (0, -1), (2, 1), (6, -1), (2, 2), (6, -2))


class Ring:
    size = 8

    def __init__(self, plan, slot, send, recv, place):
        self.plan, self.slot, self.send, self.recv, self.place = plan, slot, send, recv, place
        self.copies = {}

    def go(self, s, only=None):
        for source, step in self.plan:
            if source == s and (only is None or abs(step) == only):
                to = (s + step) % self.size
                half = None if to != self.size // 2 else (0 if step > 0 else 1)
                sem = self.size if half == 1 else to
                copy = remote(
                    self.slot(s, half), self.slot(to, half), self.send.at[sem], self.recv.at[sem],
                    *self.place(step),
                )
                copy.start()
                self.copies[sem] = copy

    def arrived(self, s):
        for sem in (s, self.size) if s == self.size // 2 else (s,):
            self.copies[sem].wait_recv()

    def finish(self):
        for sem, copy in self.copies.items():
            copy.wait_send()


class ShortRing(Ring):
    size = 4


class Pair:
    def __init__(self, mine, theirs, send, recv, other):
        self.mine, self.theirs, self.send, self.recv, self.other = mine, theirs, send, recv, other
        self.copies = {}

    def go(self, s):
        copy = remote(self.mine(s), self.theirs(s), self.send.at[s], self.recv.at[s], *self.other)
        copy.start()
        self.copies[s] = copy

    def arrived(self, s):
        self.copies[s].wait_recv()

    def finish(self):
        for sem, copy in self.copies.items():
            copy.wait_send()


def kernel(
    tokens, flags, lens, embed, gain, wqkv, wout, out,
    tokin, flagin, lenin, embedin, gainin, gain32, tok, w, kv, q, numer, den, redo, redi, att, wb, acc, ssq, segq, segk,
    local, ysend, yrecv, bsend, brecv, zsend, zrecv, qsend, qrecv, rsend, rrecv,
    asend, arecv, csend, crecv, was, war, wbs, wbr, wcs, wcr,
):
    dp, seq = lax.axis_index("dp"), lax.axis_index("seq")
    y, core = dp // 2, lax.rem(dp, 2)
    x, z = seq // NZ, lax.rem(seq, NZ)

    loads = [
        pltpu.make_async_copy(there, here, local.at[i])
        for i, (there, here) in enumerate(
            [(tokens, tokin), (flags, flagin), (embed, embedin), (gain, gainin), (lens, lenin), (wqkv, w)]
        )
    ]

    def dp_at(dy, c):
        return lax.rem(y + dy + NY, NY) * 2 + c

    def seq_at(dx, dz):
        return lax.rem(x + dx + NX, NX) * NZ + lax.rem(z + dz + NZ, NZ)

    barrier = pltpu.get_barrier_semaphore()

    @pl.loop(1, HEADS)
    def _(k):
        pl.semaphore_signal(
            barrier, inc=1, device_id=(lax.rem(dp + k, HEADS), seq), device_id_type=pl.DeviceIdType.MESH
        )

    @pl.loop(1, NZ)
    def _(k):
        pl.semaphore_signal(barrier, inc=1, device_id=(dp, seq_at(0, k)), device_id_type=pl.DeviceIdType.MESH)

    @pl.loop(1, NX)
    def _(k):
        pl.semaphore_signal(barrier, inc=1, device_id=(dp, seq_at(k, 0)), device_id_type=pl.DeviceIdType.MESH)

    for load in loads:
        load.start()
    for load in loads[:3]:
        load.wait()
    embed_row = jnp.concatenate([embedin[0:1, :], embedin[1:2, :]], axis=1).astype(F32)
    for c in range(ROWS // HD):
        rows = pl.ds(c * HD, HD)
        flag = jnp.transpose(jnp.broadcast_to(flagin[c : c + 1, :].astype(F32), (HD, HD)))
        flag = jnp.concatenate([flag, flag], axis=1)
        masked = jnp.where(flag == 1.0, embed_row, tokin[rows, :].astype(F32))
        tok[0, 0, rows, :] = masked.astype(BF16)

    pl.semaphore_wait(barrier, HEADS - 1 + NZ - 1 + NX - 1)

    def along_y(step):
        return dp_at(step, core), seq

    def along_z(step):
        return dp, seq_at(0, step)

    sibling = (y * 2 + 1 - core, seq)

    def along_x(step):
        return dp, seq_at(step, 0)

    def part(c, half):
        return pl.ds(c * R, R) if half is None else pl.ds(c * R + half * H, H)

    token_ring = [
        Ring(TREE, lambda s, half, c=c: tok.at[0, s, part(c, half)], ysend.at[c], yrecv.at[c], along_y)
        for c in range(NC)
    ]
    token_pair = [
        Pair(lambda s, c=c: tok.at[0, s, part(c, None)], lambda s, c=c: tok.at[1, s, part(c, None)],
             bsend.at[c], brecv.at[c], sibling)
        for c in range(NC)
    ]
    kv_ring = [
        Ring(TREE, lambda s, half, c=c: kv.at[s, part(c, half)], zsend.at[c], zrecv.at[c], along_z)
        for c in range(NC)
    ]
    att_ring = [
        Ring(TREE, lambda s, half, c=c: att.at[0, s, part(c, half)], asend.at[c], arecv.at[c], along_y)
        for c in range(NC)
    ]
    att_pair = [
        Pair(lambda s, c=c: att.at[0, s, part(c, None)], lambda s, c=c: att.at[1, s, part(c, None)],
             csend.at[c], crecv.at[c], sibling)
        for c in range(NC)
    ]

    def weight_part(s, half):
        return wb.at[s] if half is None else wb.at[s, pl.ds(half * (NZ // 2), NZ // 2)]

    weight_ring = ShortRing(CROSS, weight_part, wcs, wcr, along_x)

    turn = lax.rem(x - dp + HEADS, NX)

    def out_tile(d):
        return wout.at[0, pl.ds(pl.multiple_of(z * 16, 16), 16), pl.ds(pl.multiple_of(d * FEAT, FEAT), FEAT)]

    def first_hop(i):
        d = NX * i + turn
        return remote(out_tile(d), wb.at[0, z, dp // NX], was.at[i], war.at[dp // NX], d, seq)

    own_tile = pltpu.make_async_copy(out_tile(dp), wb.at[0, z, dp // NX], local.at[6])

    def second_hop(k):
        return remote(wb.at[0, z], wb.at[0, z], wbs.at[k], wbr.at[k], dp, seq_at(0, k))


    def start_first():
        for i in range(HEADS // NX):
            @pl.when(NX * i + turn != dp)
            def _():
                first_hop(i).start()

            @pl.when(NX * i + turn == dp)
            def _():
                own_tile.start()

    def finish_first():
        for i in range(HEADS // NX):
            @pl.when(NX * i + turn != dp)
            def _():
                remote(out_tile(dp), wb.at[0, z, i], was.at[i], war.at[i], NX * i + turn, seq).wait_recv()

            @pl.when(NX * i + turn == dp)
            def _():
                own_tile.wait()

    def start_second():
        finish_first()

        @pl.loop(1, NZ)
        def _(k):
            second_hop(k).start()

    def finish_hops():
        for i in range(HEADS // NX):
            @pl.when(NX * i + turn != dp)
            def _():
                first_hop(i).wait_send()

        @pl.loop(1, NZ)
        def _(k):
            second_hop(k).wait_send()

    def start_third():
        @pl.loop(1, NZ)
        def _(k):
            second_hop(k).wait_recv()

        weight_ring.go(0)

    def project(o, s, c):
        rows = pl.ds(c * R, R)
        f = dp_at(-s, core if o == 0 else 1 - core)
        values = tok[o, s, rows, :].astype(F32)
        squares = values * values
        squares = squares[:, :HD] + squares[:, HD:]
        gains = jnp.concatenate([gain32[pl.ds(2 * f, 1), :], gain32[pl.ds(2 * f + 1, 1), :]], axis=1)
        scaled = (values * gains).astype(BF16)
        product = jnp.dot(
            scaled, w[pl.ds(pl.multiple_of(f * FEAT, FEAT), FEAT), :], preferred_element_type=F32
        )
        if (o, s) == (0, 0):
            ssq[rows, :] = squares
            acc[rows, :] = product
        else:
            ssq[rows, :] += squares
            acc[rows, :] += product

    q_copies = {}

    def projected(c):
        rows = pl.ds(c * R, R)
        total = jnp.sum(ssq[rows, :], axis=1, keepdims=True)
        inv_rms = lax.rsqrt(total / D + 1e-05)
        kv[0, rows, :] = (acc[rows, HD:] * inv_rms).astype(BF16)
        kv_ring[c].go(0)
        q[0, rows, :] = (acc[rows, :HD] * inv_rms).astype(BF16)
        for k in (2, 1, 3):
            copy = remote(q.at[0, rows], q.at[k, rows], qsend.at[c, k], qrecv.at[c, k], dp, seq_at(k, 0))
            copy.start()
            q_copies[c, k] = copy

    def attend(places, rows, s, c):
        keys = pl.ds(c * R, R)
        queries = q[places, rows, :]
        shape = queries.shape
        scores = lax.dot_general(
            queries.reshape(-1, HD), kv[s, keys, :HD], (((1,), (1,)), ((), ())), preferred_element_type=F32
        )
        same = segq[places, rows, :].reshape(-1, HD) == segk[s, 0:1, keys]
        weights = jnp.where(same, jnp.exp2(scores * SCALE), 0.0)
        product = jnp.dot(weights.astype(BF16), kv[s, keys, HD:], preferred_element_type=F32)
        if (s, c) == (0, 0):
            numer[places, rows, :] = product.reshape(shape)
            den[places, rows, :] = weights.reshape(shape)
        else:
            numer[places, rows, :] += product.reshape(shape)
            den[places, rows, :] += weights.reshape(shape)

    def tokens_in(c, slots):
        for t in slots:
            token_ring[c].arrived(t)
            token_ring[c].go(t)
            token_pair[c].go(t)

    def project_mine(c, slots):
        for t in slots:
            project(0, t, c)

    def project_theirs(c, slots):
        for t in slots:
            token_pair[c].arrived(t)
            project(1, t, c)

    def keys_in(c, slots):
        for t in slots:
            kv_ring[c].arrived(t)
            kv_ring[c].go(t)

    def queries_in(c):
        for k in range(1, NX):
            q_copies[c, k].wait_recv()

    def attend_all(chunks, slots, c):
        for t in slots:
            for qc in chunks:
                attend(slice(None), pl.ds(qc * R, R), t, c)

    def mix(o, s, c):
        rows = pl.ds(c * R, R)
        h = dp_at(-s, core if o == 0 else 1 - core)
        weight = wb[lax.rem(x - h - dp + 2 * HEADS, NX), :, h // NX].reshape(HD, FEAT)
        product = jnp.dot(att[o, s, rows, :], weight, preferred_element_type=F32)
        if (o, s) == (0, 0):
            acc[rows, :FEAT] = product
        else:
            acc[rows, :FEAT] += product

    def segments():
        loads[3].wait()
        gain32[...] = gainin[...].astype(F32)
        loads[4].wait()
        lane = lax.broadcasted_iota(jnp.int32, (HD, HD), 1)
        row = lax.broadcasted_iota(jnp.int32, (HD, HD), 0)
        lens_lane = jnp.concatenate([lenin[...].astype(F32), jnp.zeros((1, HD - DOCS), F32)], axis=1)
        lens_lane = jnp.broadcast_to(lens_lane, (HD, HD))
        lens_row = jnp.transpose(lens_lane)
        ends_lane = jnp.sum(jnp.where(row <= lane, lens_row, 0.0), axis=0, keepdims=True)
        ends_row = jnp.sum(jnp.where(lane <= row, lens_lane, 0.0), axis=1, keepdims=True)
        for s in range(NX):
            base = seq_at(-s, 0) * ROWS
            position = (lax.broadcasted_iota(jnp.int32, (ROWS, HD), 0) + base).astype(F32)
            count = jnp.sum(jnp.where(position >= ends_lane, 1.0, 0.0), axis=1, keepdims=True)
            segq[s] = jnp.broadcast_to(count, (ROWS, HD))
        for s in range(NZ):
            base = seq_at(0, -s) * ROWS
            position = (lax.broadcasted_iota(jnp.int32, (HD, ROWS), 1) + base).astype(F32)
            count = jnp.sum(jnp.where(position >= ends_row, 1.0, 0.0), axis=0, keepdims=True)
            segk[s] = jnp.broadcast_to(count, (8, ROWS))


    r_copies = {}

    def send_sums(k, c):
        rows = pl.ds(c * R, R)
        redo[k, c, :R, :] = numer[k, rows, :].astype(BF16)
        left = jnp.sum(jnp.transpose(den[k, rows, :]), axis=0, keepdims=True)
        at = lax.broadcasted_iota(jnp.int32, (16, HD), 0)
        terms = jnp.zeros((16, HD), F32)
        for i in range(3):
            term = left.astype(BF16).astype(F32)
            terms = jnp.where(at == i, term, terms)
            left = left - term
        redo[k, c, R:, :] = terms.astype(BF16)
        copy = remote(redo.at[k, c], redi.at[k, c], rsend.at[c, k], rrecv.at[c, k], dp, seq_at(-k, 0))
        copy.start()
        r_copies[c, k] = copy

    def combine(c):
        rows = pl.ds(c * R, R)
        down = jnp.sum(jnp.transpose(den[0, rows, :]), axis=0, keepdims=True)
        top = numer[0, rows, :]
        for k in (1, 3, 2):
            r_copies[c, k].wait_recv()
            top = top + redi[k, c, :R, :].astype(F32)
            terms = redi[k, c, R:, :].astype(F32)
            down = down + (terms[0:1, :] + terms[1:2, :] + terms[2:3, :])
        down = jnp.transpose(jnp.broadcast_to(down, (HD, HD)))
        att[0, 0, rows, :] = (top / down).astype(BF16)
        att_ring[c].go(0)
        att_pair[c].go(0)

    def run():
        start_first()
        token_ring[0].go(0)
        token_ring[1].go(0, only=2)
        for c in range(NC):
            token_pair[c].go(0)
        segments()
        loads[5].wait()
        project_mine(0, (0,))
        project_theirs(0, (0,))
        tokens_in(0, (2, 6))
        token_ring[1].go(0, only=1)
        tokens_in(0, (1, 7))
        start_second()
        project_mine(0, (2, 6, 1, 7))
        project_theirs(0, (2, 6, 1, 7))
        tokens_in(1, (2, 6))
        tokens_in(0, (3, 5))
        project_mine(0, (3, 5))
        tokens_in(0, (4,))
        project_mine(0, (4,))
        project_theirs(0, (3, 5, 4))
        projected(0)
        tokens_in(1, (1, 7))
        project_mine(1, (0, 2, 6, 1, 7))
        project_theirs(1, (0, 2, 6, 1, 7))
        tokens_in(1, (3, 5))
        project_mine(1, (3, 5))
        tokens_in(1, (4,))
        project_mine(1, (4,))
        project_theirs(1, (3, 5, 4))
        projected(1)
        start_third()
        keys_in(0, (2, 6))
        queries_in(0)
        attend_all((0,), (0,), 0)
        keys_in(0, (1, 7))
        attend_all((0,), (2, 6, 1, 7), 0)
        keys_in(1, (2, 6))
        keys_in(0, (3, 5))
        attend_all((0,), (3, 5), 0)
        queries_in(1)
        attend_all((1,), (0, 2, 6, 1, 7, 3, 5), 0)
        attend_all((0, 1), (0,), 1)
        keys_in(0, (4,))
        attend_all((0, 1), (4,), 0)
        keys_in(1, (1, 7))
        attend_all((0, 1), (2, 6, 1, 7), 1)
        for k in (1, 3):
            weight_ring.arrived(k)
            weight_ring.go(k)
        for group in (*token_ring, *token_pair):
            group.finish()
        keys_in(1, (3, 5))
        attend_all((0, 1), (3, 5), 1)
        keys_in(1, (4,))
        for c in range(NC):
            attend_all((c,), (4,), 1)
            for k in (2, 1, 3):
                send_sums(k, c)
        for group in kv_ring:
            group.finish()
        for copy in q_copies.values():
            copy.wait_send()
        for c in range(NC):
            combine(c)
        weight_ring.arrived(2)

        def att_in(slots):
            for c in range(NC):
                for t in slots:
                    att_ring[c].arrived(t)
                    att_ring[c].go(t)
                    att_pair[c].go(t)

        def mix_mine(slots):
            for c in range(NC):
                for t in slots:
                    mix(0, t, c)

        def mix_theirs(slots):
            for c in range(NC):
                for t in slots:
                    att_pair[c].arrived(t)
                    mix(1, t, c)

        mix_mine((0,))
        for copy in r_copies.values():
            copy.wait_send()
        weight_ring.finish()
        finish_hops()
        att_in((2, 6))
        mix_theirs((0,))
        att_in((1, 7))
        mix_mine((2, 6, 1, 7))
        mix_theirs((2, 6, 1, 7))
        att_in((3, 5))
        mix_mine((3, 5))
        att_in((4,))
        mix_mine((4,))
        for group in att_ring:
            group.finish()
        mix_theirs((3, 5, 4))
        out[...] = acc[:, :FEAT].astype(BF16)

    run()
    for group in att_pair:
        group.finish()


def body(tokens, mask_flags, doc_lengths, mask_embed, norm_gain, qkv_weight, out_weight):
    vmem = pl.BlockSpec(memory_space=pltpu.VMEM)
    hbm = pl.BlockSpec(memory_space=pltpu.HBM)
    dma = lambda *shape: pltpu.SemaphoreType.DMA(shape)
    return pl.pallas_call(
        kernel,
        out_shape=jax.ShapeDtypeStruct((ROWS, FEAT), BF16),
        in_specs=[hbm] * 7,
        out_specs=vmem,
        scratch_shapes=[
            pltpu.VMEM((ROWS, FEAT), BF16),
            pltpu.VMEM((ROWS // HD, HD), jnp.int32),
            pltpu.VMEM((1, DOCS), jnp.int32),
            pltpu.VMEM((2, HD), F32),
            pltpu.VMEM((D // HD, HD), BF16),
            pltpu.VMEM((D // HD, HD), F32),
            pltpu.VMEM((2, NY, ROWS, FEAT), BF16),
            pltpu.VMEM((D, 3 * HD), BF16),
            pltpu.VMEM((NZ, ROWS, 2 * HD), BF16),
            pltpu.VMEM((NX, ROWS, HD), BF16),
            pltpu.VMEM((NX, ROWS, HD), F32),
            pltpu.VMEM((NX, ROWS, HD), F32),
            pltpu.VMEM((NX, NC, R + 16, HD), BF16),
            pltpu.VMEM((NX, NC, R + 16, HD), BF16),
            pltpu.VMEM((2, NY, ROWS, HD), BF16),
            pltpu.VMEM((NX, NZ, HEADS // NX, 16, FEAT), BF16),
            pltpu.VMEM((ROWS, 3 * HD), F32),
            pltpu.VMEM((ROWS, HD), F32),
            pltpu.VMEM((NX, ROWS, HD), F32),
            pltpu.VMEM((NZ, 8, ROWS), F32),
            dma(7),
            dma(NC, 9), dma(NC, 9), dma(NC, 8), dma(NC, 8),
            dma(NC, 9), dma(NC, 9), dma(NC, NX), dma(NC, NX),
            dma(NC, NX), dma(NC, NX),
            dma(NC, 9), dma(NC, 9), dma(NC, 8), dma(NC, 8),
            dma(HEADS // NX), dma(HEADS // NX), dma(NZ), dma(NZ), dma(NX + 1), dma(NX + 1),
        ],
        compiler_params=pltpu.CompilerParams(
            collective_id=0, has_side_effects=True, vmem_limit_bytes=VMEM_BYTES
        ),
        name="attention_layer",
    )(
        tokens, mask_flags.reshape(ROWS // HD, HD), doc_lengths.reshape(1, DOCS), mask_embed.astype(F32).reshape(2, HD),
        norm_gain.reshape(D // HD, HD), qkv_weight.reshape(D, 3 * HD), out_weight,
    )


def solution(mesh):
    placed = (P("seq", "dp"), P("seq"), P(), P("dp"), P(), P(None, "dp", None), P("dp", None, None))
    return jax.shard_map(
        body, mesh=mesh, in_specs=placed, out_specs=P("seq", "dp"), check_vma=False
    )
```
